256 devices in a mesh: store: 64 (over x, y_hi, z), grid: 2 (over core), row: 2 (over y_lo).
Axes of the slice: x: 4, y: 4 (y_hi: 2, y_lo: 2; y = y_hi * 2 + y_lo), z: 8, core: 2. Of those that a mesh axis runs over, the one named last changes fastest.
Arguments:
- embeddings: bfloat16 [131072, 768], P('store'), may hold values from -6 to 6
- members: int32 [4, 16384], replicated, may hold values from 0 to 131071, as said below
- order: int32 [4, 16384], replicated, may hold values from 0 to 16383, each once within a row
- sizes: int32 [4], replicated, may hold values from 8192 to 16384, as said below
Outputs:
- best: float32 [65536], P(('store', 'grid', 'row'))
The draws below stay inside these ranges and needn't reach their ends.
Inputs may be any that keep to these rules, and one draw needn't show every extreme that they name: `members`: all ids are distinct. Each cluster's slots fall into aligned blocks of 256 slots, and within each block exactly 4 ids lie in each storage shard of 2048 rows. `sizes`: one cluster fills all 16384 slots.
All inputs are finite; a program needn't handle non-finite values.
Results may differ from the reference program's by a relative error of at most 0.0012.
Values may be sent and summed in bfloat16 or wider, within the bound.
A program may use at most 128 MiB of HBM per device.

```python
import jax
import jax.numpy as jnp
from jax import lax

D = 768
MEM_DEV = 256
CLUS = 4
ROWS_DEV = 2048
ROWS = 131072
CAP = 16384
N_STORE = 64


def draw_members(key, part):
    key = jax.random.fold_in(key, 11)
    first, second = jax.random.split(key)
    blocks = 4 * N_STORE
    share = MEM_DEV // N_STORE
    row_perms = jax.vmap(lambda k: jax.random.permutation(k, ROWS_DEV))(jax.random.split(first, N_STORE))
    slot_perms = jax.vmap(lambda k: jax.random.permutation(k, MEM_DEV))(jax.random.split(second, blocks))
    source = slot_perms // share
    within = slot_perms % share
    block_ids = jnp.arange(blocks, dtype=jnp.int32)[:, None]
    local = row_perms[source, block_ids * share + within]
    ids = source * ROWS_DEV + local
    return ids.reshape(CLUS, CAP).astype(jnp.int32)


def draw_sizes(key, part):
    key = jax.random.fold_in(key, 12)
    first, second = jax.random.split(key)
    counts = jax.random.randint(first, (CLUS,), CAP // 2, CAP + 1)
    largest = jax.random.randint(second, (), 0, CLUS)
    counts = jnp.where(jnp.arange(CLUS) == largest, CAP, counts)
    return counts.astype(jnp.int32)


def level_of(own_key, shape, cuts, least, high):
    level = 1.0
    for dim, parts in cuts:
        draws = jax.random.uniform(jax.random.fold_in(jax.random.fold_in(own_key, 6), dim), (parts,), jnp.float32, least / len(cuts), high / len(cuts))
        level = level * jnp.repeat(jnp.exp(draws), shape[dim] // parts).reshape((-1,) + (1,) * (len(shape) - 1 - dim))
    return level


def centred(key, extent, scale, limit, cuts=(), kind=jnp.bfloat16):
    array = jax.random.normal(key, extent, jnp.float32) * scale
    if len(cuts) > 0:
        array = level_of(key, extent, cuts, -0.22, 0.18) * array
    return jnp.clip(array, min=-limit, max=limit).astype(kind)


def setup_inputs(seed: int = 0) -> dict:
    splits = jax.random.split(jax.random.key(seed), 5)
    embeddings = centred(splits[0], (ROWS, D), 1.0, 6.0, ((0, 64),))
    members = draw_members(jax.random.fold_in(splits[4], 71), 0)
    order = jax.vmap(lambda own: jax.random.permutation(own, CAP))(jax.random.split(splits[2], CLUS)).reshape((CLUS, CAP)).astype(jnp.int32)
    sizes = draw_sizes(jax.random.fold_in(splits[4], 71), 0)
    return {"embeddings": embeddings, "members": members, "order": order, "sizes": sizes}


def cluster_top(embeddings, ids, ranks, count):
    vector = embeddings[ids].astype(jnp.float32)
    scale = lax.rsqrt(lax.optimization_barrier(jnp.sum(vector * vector, axis=1, keepdims=True)) + 1e-06)
    unit = (vector * scale).astype(jnp.bfloat16)
    unit = lax.optimization_barrier(unit).astype(jnp.float32)
    slot_ids = jnp.arange(CAP, dtype=jnp.int32)
    valid = slot_ids < count
    block = 4 * MEM_DEV
    query_units = unit.reshape(CAP // block, block, D)
    query_ranks = ranks.reshape(CAP // block, block)

    def one_block(pair):
        queries, qrank = pair
        score = jnp.dot(queries, unit.T, preferred_element_type=jnp.float32, precision=lax.Precision.HIGHEST)
        mask = valid[None, :] & (ranks[None, :] < qrank[:, None])
        return jnp.maximum(-1.0, lax.optimization_barrier(jnp.max(jnp.where(mask, score, -1.0), axis=1)))
    top = lax.map(one_block, (query_units, query_ranks)).reshape(CAP)
    return jnp.where(valid, top, 0.0).astype(jnp.float32)

def reference(embeddings, members, order, sizes):
    results = []
    for cluster in range(CLUS):
        results.append(cluster_top(embeddings, members[cluster], order[cluster], sizes[cluster]))
    return jnp.concatenate(results, axis=0)
```

```python
import jax
import jax.numpy as jnp
from jax import lax
from jax.experimental import pallas as pl
from jax.experimental.pallas import tpu as pltpu
from jax.sharding import PartitionSpec as P

NZ_SLOTS = 10
OWN, X, W, V = 4, 10, 11, 12
N_SLOTS = 13
D = 768
MEM = 256
PIECE = 64
NEVER = float(1 << 20)
MESH = pl.DeviceIdType.MESH
F32 = jnp.float32
SLOT_AT = [((0, z), c) for z in range(-2, 3) for c in (0, 1)] + [((1, -1), 0), ((-1, -2), 0), ((2, -2), 0)]
ROW_SLOTS = (4, 6, 0, X, W, V)


def coordinates():
    store = lax.axis_index("store")
    return store // 16, (store // 8) % 2, store % 8, lax.axis_index("grid"), lax.axis_index("row")


def device(x, y_hi, z, core, y_lo):
    return (x * 16 + y_hi * 8 + z, core, y_lo)


def spread(row):
    return jnp.transpose(jnp.broadcast_to(row, (128, 128)))


def kernel(emb_hbm, members_hbm, order_hbm, sizes, out, emb, members, order, table, held, give, vec, col_ord, row_ord, col_best, row_best, part, mine, got, load_sem, send_sem, recv_sem, part_send, part_recv, route_send, route_recv):
    x, y_hi, z, core, y_lo = coordinates()
    y = y_hi * 2 + y_lo
    store = x * 16 + y_hi * 8 + z

    def at(dx, dz, other=0):
        side = core if other == 0 else 1 - core
        return device((x + dx + 4) % 4, y_hi, (z + dz + 8) % 8, side, y_lo)

    partner = device(x, 1 - y_hi, z, core, 1 - y_lo)
    greet = [at(0, 1), at(0, -1), at(1, 0), at(-1, 0), at(2, 0), at(0, 0, 1)]
    greet += [partner, device(x, y_hi, z, core, 1 - y_lo), device(x, 1 - y_hi, z, core, y_lo)]
    barrier = pltpu.get_barrier_semaphore()
    for one in greet:
        pl.semaphore_signal(barrier, inc=1, device_id=one, device_id_type=MESH)

    loads = [
        pltpu.make_async_copy(members_hbm, members, load_sem.at[0]),
        pltpu.make_async_copy(order_hbm, order, load_sem.at[1]),
        pltpu.make_async_copy(emb_hbm, emb, load_sem.at[2]),
    ]
    for one in loads:
        one.start()
    loads[0].wait()
    loads[1].wait()

    def lay(ref, cluster, where):
        for b in range(PIECE):
            line = ref[pl.ds(cluster, 1), b * MEM : (b + 1) * MEM]
            table[where, b : b + 1, :] = line
            table[where, PIECE + b : PIECE + b + 1, :] = line

    lay(members, y, 0)
    lay(members, 3 - y, 1)
    lay(order, y, 2)
    ids = jnp.transpose(table[0])
    ids_partner = jnp.transpose(table[1])
    slot = lax.broadcasted_iota(jnp.int32, (MEM, 128), 0) + MEM * (lax.broadcasted_iota(jnp.int32, (MEM, 128), 1) % PIECE)
    rank_of = jnp.where(slot < sizes[y], jnp.transpose(table[2]).astype(F32), NEVER)
    upper = lax.broadcasted_iota(jnp.int32, (1, 128), 1) // PIECE
    before = (
        lax.broadcasted_iota(jnp.int32, (MEM, MEM), 1) < lax.broadcasted_iota(jnp.int32, (MEM, MEM), 0)
    ).astype(jnp.bfloat16)

    def ranks(local):
        inside = (local >= 0) & (local < 2048)
        count = jnp.dot(before, jnp.where(inside, 1.0, 0.0).astype(jnp.bfloat16), preferred_element_type=F32)
        return jnp.where(inside, count, -1.0)

    def pick(rank, side, values):
        wanted = (2 * side + upper).astype(F32)
        return jnp.sum(jnp.where(rank == wanted, values, 0.0), axis=0, keepdims=True)

    chosen = []
    for table_ids in (ids, ids_partner):
        local = table_ids - store * 2048
        chosen.append(spread(pick(ranks(local), core, local.astype(F32))).astype(jnp.int32))
    loads[2].wait()
    lane = lax.broadcasted_iota(jnp.int32, (128, 128), 1)
    for half in range(2):
        onehot = jnp.concatenate([jnp.where(chosen[half] == lane + 128 * j, 1.0, 0.0).astype(jnp.bfloat16) for j in range(16)], axis=1)
        for n in range(3):
            vec[:, n * 256 : (n + 1) * 256] = jnp.dot(onehot, emb[:, n * 256 : (n + 1) * 256], preferred_element_type=F32)
        vector = vec[...]
        scale = lax.rsqrt(jnp.sum(vector * vector, axis=1, keepdims=True) + 1e-06)
        unit = (vector * scale).astype(jnp.bfloat16).reshape(2, PIECE, D)
        if half == 0:
            held[pl.ds(OWN * 4 + y_hi * 2, 2)] = unit
        else:
            give[...] = unit

    pl.semaphore_wait(barrier, len(greet))

    def piece(slot, q):
        half, rr = q // 2, q % 2
        side = y_hi if half == 0 else 1 - y_hi
        return slot * 4 + side * 2 + rr

    def send(src_slot, dst_slot, q, to):
        pltpu.make_async_remote_copy(
            held.at[piece(src_slot, q)],
            held.at[piece(dst_slot, q)],
            send_sem.at[0],
            recv_sem.at[dst_slot * 4 + q],
            device_id=to,
            device_id_type=MESH,
        ).start()

    def arrived(slot, q):
        one = held.at[piece(slot, q)]
        pltpu.make_async_remote_copy(
            one, one, send_sem.at[0], recv_sem.at[slot * 4 + q], device_id=at(0, 1), device_id_type=MESH
        ).wait_recv()

    def send_own(q):
        send(OWN, 2, q, at(0, 1))
        send(OWN, 6, q, at(0, -1))
        send(OWN, 5, q, at(0, 0, 1))

    def step_near(q):
        arrived(2, q)
        send(2, 0, q, at(0, 1))
        send(2, X, q, at(-1, 0))
        send(2, 3, q, at(0, 0, 1))
        arrived(6, q)
        send(6, 8, q, at(0, -1))
        send(6, 7, q, at(0, 0, 1))

    def step_far(q):
        arrived(0, q)
        send(0, W, q, at(1, 0))
        send(0, V, q, at(2, 0))
        send(0, 1, q, at(0, 0, 1))
        arrived(8, q)
        send(8, 9, q, at(0, 0, 1))

    for rr in range(2):
        pltpu.make_async_remote_copy(
            give.at[rr],
            held.at[OWN * 4 + y_hi * 2 + rr],
            send_sem.at[0],
            recv_sem.at[OWN * 4 + 2 + rr],
            device_id=partner,
            device_id_type=MESH,
        ).start()
    send_own(0)
    send_own(1)

    def block_order(dx, dz):
        rows = []
        for hi in range(2):
            shard = ((x + dx + 4) % 4) * 16 + hi * 8 + (z + dz + 8) % 8
            rows.append(ranks(ids - shard * 2048))
        return rows

    for s in range(N_SLOTS):
        (dx, dz), other = SLOT_AT[s]
        if other == 0:
            both = block_order(dx, dz)
        side = core if other == 0 else 1 - core
        for hi in range(2):
            line = pick(both[hi], side, rank_of)
            if s < NZ_SLOTS:
                col_ord[s, :, hi * 128 : (hi + 1) * 128] = jnp.broadcast_to(line, (8, 128))
            if s in ROW_SLOTS:
                row_ord[ROW_SLOTS.index(s), hi * 128 : (hi + 1) * 128, :] = spread(line)
    col_best[...] = jnp.full(col_best.shape, -1.0, F32)
    row_best[...] = jnp.full(row_best.shape, -1.0, F32)

    def product(left, right, full):
        where = ROW_SLOTS.index(left)
        a = held[left * 4 : left * 4 + 4].reshape(MEM, D)
        b = held[pl.ds(right * 4, 4)].reshape(MEM, D)
        score = lax.dot_general(a, b, (((1,), (1,)), ((), ())), preferred_element_type=F32)
        own = row_ord[where]
        own = jnp.concatenate([own, own], axis=1)
        other = col_ord[right][0:1, :]
        earlier = other < own
        for_rows = jnp.where(earlier, score, -1.0)
        row_best[where] = jnp.maximum(row_best[where], jnp.maximum(for_rows[:, :128], for_rows[:, 128:]))
        if full:
            for_cols = jnp.where(earlier, -1.0, score)
            col_best[right] = jnp.maximum(col_best[right], jnp.max(for_cols.reshape(32, 8, MEM), axis=0))

    def products(left, first, last, full):
        def one(right, carry):
            product(left, right, full)
            return carry

        lax.fori_loop(first, last, one, 0)

    step_near(0)
    step_near(1)
    arrived(OWN, 2)
    send_own(2)
    step_far(0)
    arrived(OWN, 3)
    send_own(3)
    step_far(1)
    step_near(2)
    step_near(3)
    for q in range(4):
        arrived(5, q)
    products(OWN, 4, 6, False)
    step_far(2)
    step_far(3)
    for q in range(4):
        arrived(7, q)
        arrived(9, q)
    products(OWN, 6, 10, True)
    for q in range(4):
        arrived(1, q)
    products(6, 0, 2, True)
    products(0, 8, 10, False)
    for q in range(4):
        arrived(X, q)
        arrived(3, q)
    products(X, 0, 10, True)
    for q in range(4):
        arrived(W, q)
    products(W, 4, 10, True)
    for q in range(4):
        arrived(V, q)
    products(V, 2, 8, True)
    products(V, 0, 2, False)
    products(V, 8, 10, False)

    sends = []
    for s in range(N_SLOTS):
        (dx, dz), other = SLOT_AT[s]
        for hi in range(2):
            line = jnp.full((1, 128), -1.0, F32)
            if s in ROW_SLOTS:
                line = jnp.max(jnp.transpose(row_best[ROW_SLOTS.index(s), hi * 128 : (hi + 1) * 128, :]), axis=0, keepdims=True)
            if s < NZ_SLOTS:
                line = jnp.maximum(line, jnp.max(col_best[s, :, hi * 128 : (hi + 1) * 128], axis=0, keepdims=True))
            if s == OWN:
                mine[hi : hi + 1, :] = line
            else:
                part[0, s, hi : hi + 1, :] = line
        if s != OWN:
            pltpu.make_async_remote_copy(
                part.at[0, s],
                part.at[1, s],
                part_send.at[0],
                part_recv.at[0],
                device_id=at(dx, dz, other),
                device_id_type=MESH,
            ).start()
    twelve = part.at[0, pl.ds(0, N_SLOTS - 1)]
    back = pltpu.make_async_remote_copy(twelve, twelve, part_send.at[0], part_recv.at[0], device_id=at(0, 1), device_id_type=MESH)
    back.wait_recv()
    best = mine[...]
    for s in range(N_SLOTS):
        if s != OWN:
            best = jnp.maximum(best, part[1, s])
    mine[...] = best
    back.wait_send()

    sender = (x * 8 + z) * 2 + core

    def route(b, carry):
        to_hi, to_z, to_core, to_lo = b // 32, (b // 4) % 8, (b // 2) % 2, b % 2
        self_there = (x == y) & (to_hi == y_hi) & (to_z == z) & (to_core == core) & (to_lo == y_lo)

        @pl.when(self_there)
        def _():
            pltpu.make_async_copy(mine, got.at[sender], route_recv.at[0]).start()

        @pl.when(jnp.logical_not(self_there))
        def _():
            pltpu.make_async_remote_copy(
                mine,
                got.at[sender],
                route_send.at[0],
                route_recv.at[0],
                device_id=device(y, to_hi, to_z, to_core, to_lo),
                device_id_type=MESH,
            ).start()

        return carry

    lax.fori_loop(0, 64, route, 0)

    block = ((y_hi * 8 + z) * 2 + core) * 2 + y_lo
    own_ids = members[pl.ds(x, 1), pl.ds(pl.multiple_of(block * MEM, MEM), MEM)]
    shard = own_ids // 2048
    shard_rows = jnp.concatenate([spread(shard[:, :128].astype(F32)), spread(shard[:, 128:].astype(F32))], axis=0)
    shard_rows = jnp.concatenate([shard_rows, shard_rows], axis=1)
    same = (shard_rows == shard.astype(F32)) & (
        lax.broadcasted_iota(jnp.int32, (MEM, MEM), 0) < lax.broadcasted_iota(jnp.int32, (MEM, MEM), 1)
    )
    rank = jnp.sum(jnp.where(same, 1.0, 0.0), axis=0, keepdims=True).astype(jnp.int32)
    from_sender = ((shard // 16) * 8 + shard % 8) * 2 + rank // 2
    from_place = ((shard // 8) % 2) * 2 + rank % 2
    from_which = from_sender * 4 + from_place

    total = got
    land = pltpu.make_async_remote_copy(total, total, route_send.at[0], route_recv.at[0], device_id=at(0, 1), device_id_type=MESH)
    land.wait_recv()
    value = jnp.zeros((1, MEM), F32)
    senders = lax.broadcasted_iota(jnp.int32, (64, MEM), 0)
    lanes = lax.broadcasted_iota(jnp.int32, (64, 128), 1)
    for hi in range(2):
        rows = got[:, hi, :]
        for rr in range(2):
            column = jnp.sum(jnp.where(lanes == rr * PIECE + block, rows, 0.0), axis=1, keepdims=True)
            here = from_which == senders * 4 + (hi * 2 + rr)
            value = value + jnp.sum(jnp.where(here, column, 0.0), axis=0, keepdims=True)
    slots = block * MEM + lax.broadcasted_iota(jnp.int32, (1, MEM), 1)
    out[...] = jnp.where(slots < sizes[x], value, 0.0)

    sent = held.at[pl.ds(0, 50)]
    pltpu.make_async_remote_copy(sent, sent, send_sem.at[0], recv_sem.at[0], device_id=at(0, 1), device_id_type=MESH).wait_send()

    @pl.when(x == y)
    def _():
        fewer = got.at[pl.ds(0, 63)]
        pltpu.make_async_remote_copy(fewer, fewer, route_send.at[0], route_recv.at[0], device_id=at(0, 1), device_id_type=MESH).wait_send()

    @pl.when(x != y)
    def _():
        pltpu.make_async_remote_copy(total, total, route_send.at[0], route_recv.at[0], device_id=at(0, 1), device_id_type=MESH).wait_send()


def on_device(embeddings, members, order, sizes):
    vmem = pltpu.VMEM
    dma = pltpu.SemaphoreType.DMA
    best = pl.pallas_call(
        kernel,
        out_shape=jax.ShapeDtypeStruct((1, MEM), F32),
        in_specs=[pl.BlockSpec(memory_space=pl.ANY)] * 3 + [pl.BlockSpec(memory_space=pltpu.SMEM)],
        out_specs=pl.BlockSpec(memory_space=pltpu.VMEM),
        scratch_shapes=[
            vmem((2048, D), jnp.bfloat16),
            vmem((4, 16384), jnp.int32),
            vmem((4, 16384), jnp.int32),
            vmem((3, 128, MEM), jnp.int32),
            vmem((N_SLOTS * 4, PIECE, D), jnp.bfloat16),
            vmem((2, PIECE, D), jnp.bfloat16),
            vmem((128, D), F32),
            vmem((NZ_SLOTS, 8, MEM), F32),
            vmem((len(ROW_SLOTS), MEM, 128), F32),
            vmem((NZ_SLOTS, 8, MEM), F32),
            vmem((len(ROW_SLOTS), MEM, 128), F32),
            vmem((2, N_SLOTS, 2, 128), F32),
            vmem((2, 128), F32),
            vmem((64, 2, 128), F32),
            dma((3,)),
            dma((1,)),
            dma((N_SLOTS * 4,)),
            dma((1,)),
            dma((1,)),
            dma((1,)),
            dma((1,)),
        ],
        compiler_params=pltpu.CompilerParams(collective_id=0, has_side_effects=True, vmem_limit_bytes=48 << 20),
        cost_estimate=pl.CostEstimate(flops=8 << 30, bytes_accessed=8 << 20, transcendentals=0),
    )(embeddings, members, order, sizes)
    return best.reshape(MEM)


def solution(mesh):
    return jax.shard_map(
        on_device,
        mesh=mesh,
        in_specs=(P("store", None), P(), P(), P()),
        out_specs=P(("store", "grid", "row")),
        check_vma=False,
    )
```

```python
import jax
import jax.numpy as jnp
from jax import lax
from jax.experimental import pallas as pl
from jax.experimental.pallas import tpu as pltpu
from jax.sharding import PartitionSpec as P

AT = [(0, 0), (0, -2), (0, -1), (0, 1), (0, 2), (1, -2), (1, -1), (2, -2), (-1, -1)]
ROUTE = [(5, 5, 5, 5, 5, 5, 5, 5), (0, 0, 0, 0, 0, 0, 0, 0), (0, 0, 0, 0, 0, 0, 0, 0), (3, 3, 3, 3, 3, 3, 3, 3), (6, 6, 6, 6, 6, 6, 6, 6), (2, 2, 2, 2, 2, 2, 2, 2), (5, 5, 5, 5, 5, 5, 5, 5), (2, 2, 2, 2, 2, 2, 2, 2)]
PROGRAM = [
    ("piece", 0, 4),
    ("piece", 2, 0),
    ("piece", 3, 0),
    ("piece", 0, 5),
    ("piece", 2, 3),
    ("piece", 3, 3),
    ("piece", 0, 6),
    ("piece", 2, 2),
    ("piece", 3, 2),
    ("piece", 0, 7),
    ("piece", 2, 1),
    ("piece", 3, 1),
    ("piece", 6, 0),
    ("piece", 8, 0),
    ("piece", 2, 4),
    ("piece", 4, 0),
    ("piece", 6, 3),
    ("piece", 8, 3),
    ("piece", 2, 5),
    ("piece", 4, 3),
    ("piece", 6, 2),
    ("piece", 8, 2),
    ("piece", 2, 6),
    ("piece", 3, 6),
    ("twin", 0, 0),
    ("twin", 0, 1),
    ("products", ((0, 0, False),)),
    ("piece", 6, 1),
    ("piece", 8, 1),
    ("piece", 2, 7),
    ("piece", 4, 2),
    ("products", ((2, 0, True),)),
    ("piece", 6, 4),
    ("piece", 8, 4),
    ("piece", 4, 1),
    ("piece", 5, 0),
    ("piece", 6, 5),
    ("piece", 8, 5),
    ("piece", 3, 4),
    ("piece", 5, 3),
    ("piece", 6, 6),
    ("piece", 8, 6),
    ("piece", 4, 6),
    ("piece", 5, 2),
    ("piece", 6, 7),
    ("piece", 8, 7),
    ("products", ((6, 0, True),)),
    ("piece", 3, 5),
    ("piece", 5, 1),
    ("twin", 2, 0),
    ("twin", 2, 1),
    ("products", ((6, 2, True),)),
    ("piece", 1, 0),
    ("piece", 7, 0),
    ("known",),
    ("piece", 3, 7),
    ("piece", 5, 4),
    ("products", ((8, 0, True),)),
    ("piece", 1, 3),
    ("piece", 7, 3),
    ("products", ((3, 2, True),)),
    ("piece", 4, 4),
    ("piece", 5, 5),
    ("piece", 1, 2),
    ("piece", 7, 2),
    ("twin", 8, 0),
    ("twin", 8, 1),
    ("products", ((3, 8, True),)),
    ("piece", 5, 6),
    ("products", ((6, 8, False),)),
    ("piece", 1, 1),
    ("piece", 4, 5),
    ("piece", 7, 1),
    ("piece", 5, 7),
    ("twin", 3, 0),
    ("twin", 3, 1),
    ("products", ((6, 3, True),)),
    ("piece", 1, 4),
    ("piece", 4, 7),
    ("piece", 7, 4),
    ("products", ((5, 3, True), (5, 8, True))),
    ("piece", 1, 5),
    ("piece", 7, 5),
    ("products", ((4, 2, True), (4, 8, True))),
    ("piece", 1, 6),
    ("piece", 7, 6),
    ("twin", 5, 0),
    ("twin", 5, 1),
    ("products", ((4, 5, True),)),
    ("piece", 1, 7),
    ("piece", 7, 7),
    ("twin", 4, 0),
    ("twin", 4, 1),
    ("products", ((1, 4, False), (7, 0, True), (7, 3, True), (7, 4, False))),
]
D = 768
MEM = 256
BLOCKS = 64
PIECES = len(ROUTE[0])
HALF = PIECES // 2
ROWS = MEM // PIECES
NEVER = float(1 << 20)
MESH = pl.DeviceIdType.MESH
F32 = jnp.float32
N_SLOTS = len(AT)
PRODUCTS = [one for step in PROGRAM if step[0] == "products" for one in step[1]]
LEFT = sorted({one[0] for one in PRODUCTS})
RIGHT = sorted({one[1] for one in PRODUCTS})
BASE = [s + sum(r < s for r in RIGHT) for s in range(N_SLOTS)]
N_HELD = N_SLOTS + len(RIGHT)
PARTS = [(AT[s], 0) for s in LEFT] + [(AT[s], other) for s in RIGHT for other in (0, 1)]
STEPS = {tuple((a - b) for a, b in zip(AT[s], AT[ROUTE[s - 1][q]])) for s in range(1, N_SLOTS) for q in range(PIECES)}
N_SENT = PIECES * (N_SLOTS - 1) + PIECES * len(RIGHT) + HALF


def coordinates():
    store = lax.axis_index("store")
    return store // 16, (store // 8) % 2, store % 8, lax.axis_index("grid"), lax.axis_index("row")


def device(x, y_hi, z, core, y_lo):
    return (x * 16 + y_hi * 8 + z, core, y_lo)


def spread(row):
    return jnp.transpose(jnp.broadcast_to(row, (128, 128)))


def lookup(n, values):
    if len(set(values)) == 1:
        return values[0]
    found = jnp.int32(values[0])
    for k in range(1, len(values)):
        if values[k] != values[0]:
            found = jnp.where(n == k, jnp.int32(values[k]), found)
    return found


def kernel(emb_hbm, members_hbm, order_hbm, sizes_hbm, out, sizes, emb, members, order, table, held, give, vec, col_ord, row_ord, col_best, row_best, lines, tell, got, swap, load_sem, send_sem, recv_sem, twin_sem, route_send, route_recv, known):
    x, y_hi, z, core, y_lo = coordinates()
    y = y_hi * 2 + y_lo
    store = x * 16 + y_hi * 8 + z

    def at(dx, dz, other=0, across=False):
        side = core if other == 0 else 1 - core
        if across:
            return device((x + dx + 4) % 4, 1 - y_hi, (z + dz + 8) % 8, side, 1 - y_lo)
        return device((x + dx + 4) % 4, y_hi, (z + dz + 8) % 8, side, y_lo)

    near = sorted({((sign * dx) % 4, (sign * dz) % 8) for dx, dz in STEPS for sign in (1, -1)})
    greet = [at(dx, dz) for dx, dz in near] + [at(0, 0, 0, True), at(0, 0, 1)]
    greet += [device(x, y_hi, z, core, 1 - y_lo), device(x, 1 - y_hi, z, core, y_lo)]
    barrier = pltpu.get_barrier_semaphore()
    for one in greet:
        pl.semaphore_signal(barrier, inc=1, device_id=one, device_id_type=MESH)

    loads = [
        pltpu.make_async_copy(members_hbm, members, load_sem.at[0]),
        pltpu.make_async_copy(order_hbm, order, load_sem.at[1]),
        pltpu.make_async_copy(emb_hbm, emb, load_sem.at[2]),
        pltpu.make_async_copy(sizes_hbm, sizes, load_sem.at[3]),
    ]
    for one in loads:
        one.start()
    loads[0].wait()

    def lay(ref, cluster, where):
        for b in range(BLOCKS):
            line = ref[pl.ds(cluster, 1), b * MEM : (b + 1) * MEM]
            table[where, b : b + 1, :] = line
            table[where, BLOCKS + b : BLOCKS + b + 1, :] = line

    lay(members, y, 0)
    lay(members, 3 - y, 1)
    ids = jnp.transpose(table[0])
    ids_partner = jnp.transpose(table[1])
    upper = lax.broadcasted_iota(jnp.int32, (1, 128), 1) // BLOCKS
    before = (
        lax.broadcasted_iota(jnp.int32, (MEM, MEM), 1) < lax.broadcasted_iota(jnp.int32, (MEM, MEM), 0)
    ).astype(jnp.bfloat16)

    def ranks(local):
        inside = (local >= 0) & (local < 2048)
        count = jnp.dot(before, jnp.where(inside, 1.0, 0.0).astype(jnp.bfloat16), preferred_element_type=F32)
        return jnp.where(inside, count, -1.0)

    def pick(rank, side, values):
        wanted = (2 * side + upper).astype(F32)
        return jnp.sum(jnp.where(rank == wanted, values, 0.0), axis=0, keepdims=True)

    chosen = []
    for table_ids in (ids_partner, ids):
        local = table_ids - store * 2048
        chosen.append(spread(pick(ranks(local), core, local.astype(F32))).astype(jnp.int32))
    loads[2].wait()
    lane = lax.broadcasted_iota(jnp.int32, (128, 128), 1)
    for half in range(2):
        onehot = jnp.concatenate([jnp.where(chosen[half] == lane + 128 * j, 1.0, 0.0).astype(jnp.bfloat16) for j in range(16)], axis=1)
        for n in range(3):
            vec[:, n * 256 : (n + 1) * 256] = jnp.dot(onehot, emb[:, n * 256 : (n + 1) * 256], preferred_element_type=F32)
        vector = vec[...]
        scale = lax.rsqrt(jnp.sum(vector * vector, axis=1, keepdims=True) + 1e-06)
        unit = (vector * scale).astype(jnp.bfloat16).reshape(HALF, ROWS, D)
        if half == 0:
            give[...] = unit
        else:
            held[pl.ds(y_hi * HALF, HALF)] = unit

    pl.semaphore_wait(barrier, len(greet))

    def side_of(half):
        return y_hi if half == 0 else 1 - y_hi

    def piece(slot, q):
        return BASE[slot] * PIECES + side_of(q // HALF) * HALF + q % HALF

    def push(src, dst, sem, to):
        pltpu.make_async_remote_copy(src, dst, send_sem.at[0], sem, device_id=to, device_id_type=MESH).start()

    def landed(ref, sem):
        pltpu.make_async_remote_copy(ref, ref, send_sem.at[0], sem, device_id=at(0, 0, 1), device_id_type=MESH).wait_recv()

    def forward(slot, q):
        for s in range(1, N_SLOTS):
            if ROUTE[s - 1][q] == slot:
                push(held.at[piece(slot, q)], held.at[piece(s, q)], recv_sem.at[s * PIECES + q], at(AT[slot][0] - AT[s][0], AT[slot][1] - AT[s][1]))

    def twin(slot, half):
        if slot in RIGHT:
            where = BASE[slot] * PIECES + side_of(half) * HALF
            push(held.at[pl.ds(where, HALF)], held.at[pl.ds(where + PIECES, HALF)], twin_sem.at[slot * 2 + half], at(0, 0, 1))

    for q in range(HALF):
        push(give.at[q], held.at[y_hi * HALF + q], recv_sem.at[HALF + q], at(0, 0, 0, True))
        forward(0, q)
    twin(0, 0)

    loads[1].wait()
    loads[3].wait()
    lay(order, y, 2)
    slot = lax.broadcasted_iota(jnp.int32, (MEM, 128), 0) + MEM * (lax.broadcasted_iota(jnp.int32, (MEM, 128), 1) % BLOCKS)
    rank_of = jnp.where(slot < sizes[y], jnp.transpose(table[2]).astype(F32), NEVER)
    for s in range(N_SLOTS):
        for hi in range(2):
            shard = ((x + AT[s][0] + 4) % 4) * 16 + hi * 8 + (z + AT[s][1] + 8) % 8
            rank = ranks(ids - shard * 2048)
            line = pick(rank, core, rank_of)
            if s in LEFT:
                row_ord[LEFT.index(s), hi * 128 : (hi + 1) * 128, :] = spread(line)
            if s in RIGHT:
                r = RIGHT.index(s)
                col_ord[r, :, hi * 128 : (hi + 1) * 128] = jnp.broadcast_to(line, (8, 128))
                line = pick(rank, 1 - core, rank_of)
                col_ord[r, :, 256 + hi * 128 : 256 + (hi + 1) * 128] = jnp.broadcast_to(line, (8, 128))
    col_best[...] = jnp.full(col_best.shape, -1.0, F32)
    row_best[...] = jnp.full(row_best.shape, -1.0, F32)

    def products(group):
        def one(n, carry):
            left = lookup(n, [LEFT.index(a) for a, b, full in group])
            left_at = lookup(n, [BASE[a] * PIECES for a, b, full in group])
            right = lookup(n, [RIGHT.index(b) for a, b, full in group])
            right_at = lookup(n, [BASE[b] * PIECES for a, b, full in group])
            column = lookup(n, [RIGHT.index(b) if full else len(RIGHT) for a, b, full in group])
            a = held[pl.ds(left_at, PIECES)].reshape(MEM, D)
            b = held[pl.ds(right_at, 2 * PIECES)].reshape(2 * MEM, D)
            score = lax.dot_general(a, b, (((1,), (1,)), ((), ())), preferred_element_type=F32)
            own = row_ord[left]
            best = row_best[left]
            for part in range(4):
                lanes = slice(part * 128, (part + 1) * 128)
                mine = score[:, lanes]
                earlier = col_ord[right, 0:1, lanes] < own
                best = jnp.maximum(best, jnp.where(earlier, mine, -1.0))
                later = jnp.max(jnp.where(earlier, -1.0, mine).reshape(32, 8, 128), axis=0)
                col_best[column, :, lanes] = jnp.maximum(col_best[column, :, lanes], later)
            row_best[left] = best
            return carry

        if len(group) == 1:
            one(0, 0)
        else:
            lax.fori_loop(0, len(group), one, 0)

    for step in PROGRAM:
        if step[0] == "piece":
            s, q = step[1:]
            landed(held.at[piece(s, q)], recv_sem.at[s * PIECES + q])
            forward(s, q)
            half = {("piece", s, r) for r in range(PIECES) if r // HALF == q // HALF}
            if half <= set(PROGRAM[: PROGRAM.index(step) + 1]):
                twin(s, q // HALF)
        elif step[0] == "known":
            for s in range(N_SLOTS):
                for other in (0, 1):
                    if s > 0 or other > 0:
                        pl.semaphore_signal(known, inc=1, device_id=at(AT[s][0], AT[s][1], other), device_id_type=MESH)
        elif step[0] == "twin":
            s, half = step[1:]
            landed(held.at[pl.ds(BASE[s] * PIECES + PIECES + side_of(half) * HALF, HALF)], twin_sem.at[s * 2 + half])
        else:
            products(step[1])

    for p in range(len(PARTS)):
        for hi in range(2):
            if p < len(LEFT):
                line = jnp.max(jnp.transpose(row_best[p, hi * 128 : (hi + 1) * 128, :]), axis=0, keepdims=True)
            else:
                r, other = (p - len(LEFT)) // 2, (p - len(LEFT)) % 2
                line = jnp.max(col_best[r, :, other * 256 + hi * 128 : other * 256 + (hi + 1) * 128], axis=0, keepdims=True)
            lines[p * 2 + hi : p * 2 + hi + 1, :] = line
    turned = jnp.transpose(lines[...])
    tell[:, 0, :] = turned[:BLOCKS]
    tell[:, 1, :] = turned[BLOCKS:]

    pl.semaphore_wait(known, 2 * N_SLOTS - 1)

    sender = (x * 8 + z) * 2 + core
    home = (y_hi * 8 + z) * 4 + core * 2 + y_lo

    def route(n, carry):
        b = lax.rem(home + n, 64)
        pltpu.make_async_remote_copy(
            tell.at[b],
            got.at[sender],
            route_send.at[0],
            route_recv.at[0],
            device_id=(y * 16 + b // 4, (b // 2) % 2, b % 2),
            device_id_type=MESH,
        ).start()
        return carry

    @pl.when(x == y)
    def _():
        pltpu.make_async_copy(tell.at[home], got.at[sender], route_recv.at[0]).start()

    @pl.when(x != y)
    def _():
        route(0, 0)

    lax.fori_loop(1, 64, route, 0)

    block = home
    own_ids = members[pl.ds(x, 1), pl.ds(pl.multiple_of(block * MEM, MEM), MEM)]
    shard = own_ids // 2048
    shard_rows = jnp.concatenate([spread(shard[:, :128].astype(F32)), spread(shard[:, 128:].astype(F32))], axis=0)
    shard_rows = jnp.concatenate([shard_rows, shard_rows], axis=1)
    same = (shard_rows == shard.astype(F32)) & (
        lax.broadcasted_iota(jnp.int32, (MEM, MEM), 0) < lax.broadcasted_iota(jnp.int32, (MEM, MEM), 1)
    )
    rank = jnp.sum(jnp.where(same, 1.0, 0.0), axis=0, keepdims=True).astype(jnp.int32)
    from_sender = ((shard // 16) * 8 + shard % 8) * 2 + rank // 2
    from_place = (rank % 2) * 2 + (shard // 8) % 2
    from_which = from_sender * 4 + from_place
    slots = block * MEM + lax.broadcasted_iota(jnp.int32, (1, MEM), 1)
    in_use = slots < sizes[x]
    lane_z = lax.broadcasted_iota(jnp.int32, (4, 128), 1) % 16
    senders = lax.broadcasted_iota(jnp.int32, (64, MEM), 0)

    pltpu.make_async_remote_copy(got, got, route_send.at[0], route_recv.at[0], device_id=at(0, 0, 1), device_id_type=MESH).wait_recv()
    for rr in range(2):
        heard = got[:, rr, :]
        swap[rr] = jnp.transpose(jnp.concatenate([heard, heard], axis=0))
    value = jnp.full((4, 128), -1.0, F32)
    for p in range(len(PARTS)):
        (dx, dz), other = PARTS[p]
        rows = jnp.concatenate([swap[0, 2 * p : 2 * p + 2, :], swap[1, 2 * p : 2 * p + 2, :]], axis=0)
        if dx % 4 or dz % 8:
            turn = 16 * (dx % 4) + 2 * (dz % 8)
            moved = pltpu.roll(rows, turn, 1)
            if dz % 8:
                moved = jnp.where(lane_z >= 2 * (dz % 8), moved, pltpu.roll(rows, (turn - 16) % 128, 1))
            rows = moved
        if other:
            rows = jnp.where(lane_z % 2 == 0, pltpu.roll(rows, 127, 1), pltpu.roll(rows, 1, 1))
        value = jnp.maximum(value, rows)
    final = jnp.zeros((1, MEM), F32)
    for place in range(4):
        column = spread(value[place : place + 1, :])[:64]
        column = jnp.concatenate([column, column], axis=1)
        here = from_which == senders * 4 + place
        final = final + jnp.sum(jnp.where(here, column, 0.0), axis=0, keepdims=True)
    out[...] = jnp.where(in_use, final, 0.0)

    sent = held.at[pl.ds(0, N_SENT)]
    pltpu.make_async_remote_copy(sent, sent, send_sem.at[0], recv_sem.at[0], device_id=at(0, 0, 1), device_id_type=MESH).wait_send()

    @pl.when(x == y)
    def _():
        fewer = got.at[pl.ds(0, 63)]
        pltpu.make_async_remote_copy(fewer, fewer, route_send.at[0], route_recv.at[0], device_id=at(0, 0, 1), device_id_type=MESH).wait_send()

    @pl.when(x != y)
    def _():
        pltpu.make_async_remote_copy(got, got, route_send.at[0], route_recv.at[0], device_id=at(0, 0, 1), device_id_type=MESH).wait_send()


def on_device(embeddings, members, order, sizes):
    vmem = pltpu.VMEM
    dma = pltpu.SemaphoreType.DMA
    best = pl.pallas_call(
        kernel,
        out_shape=jax.ShapeDtypeStruct((1, MEM), F32),
        in_specs=[pl.BlockSpec(memory_space=pltpu.HBM)] * 4,
        out_specs=pl.BlockSpec(memory_space=pltpu.VMEM),
        scratch_shapes=[
            pltpu.SMEM((4,), jnp.int32),
            vmem((2048, D), jnp.bfloat16),
            vmem((4, 16384), jnp.int32),
            vmem((4, 16384), jnp.int32),
            vmem((3, 128, MEM), jnp.int32),
            vmem((max(N_HELD * PIECES, N_SENT), ROWS, D), jnp.bfloat16),
            vmem((HALF, ROWS, D), jnp.bfloat16),
            vmem((128, D), F32),
            vmem((len(RIGHT), 8, 512), F32),
            vmem((len(LEFT), MEM, 128), F32),
            vmem((len(RIGHT) + 1, 8, 512), F32),
            vmem((len(LEFT), MEM, 128), F32),
            vmem((128, 128), F32),
            vmem((64, 2, 128), F32),
            vmem((64, 2, 128), F32),
            vmem((2, 128, 128), F32),
            dma((4,)),
            dma((1,)),
            dma((N_SLOTS * PIECES,)),
            dma((N_SLOTS * 2,)),
            dma((1,)),
            dma((1,)),
            pltpu.SemaphoreType.REGULAR,
        ],
        compiler_params=pltpu.CompilerParams(collective_id=0, has_side_effects=True, vmem_limit_bytes=64 << 20),
        cost_estimate=pl.CostEstimate(flops=8 << 30, bytes_accessed=8 << 20, transcendentals=0),
    )(embeddings, members, order, sizes)
    return best.reshape(MEM)


def solution(mesh):
    return jax.shard_map(
        on_device,
        mesh=mesh,
        in_specs=(P("store", None), P(), P(), P()),
        out_specs=P(("store", "grid", "row")),
        check_vma=False,
    )
```

```python
import jax
import jax.numpy as jnp
from jax import lax
from jax.experimental import pallas as pl
from jax.experimental.pallas import tpu as pltpu
from jax.sharding import PartitionSpec as P

AT = [(0, 0), (0, -2), (0, -1), (0, 1), (0, 2), (1, -2), (1, -1), (2, -2), (-1, -1)]
ROUTE = [(5, 5, 5, 5, 5, 5, 5, 5), (0, 0, 0, 0, 0, 0, 0, 0), (0, 0, 0, 0, 0, 0, 0, 0), (3, 3, 3, 3, 3, 3, 3, 3), (6, 6, 6, 6, 6, 6, 6, 6), (2, 2, 2, 2, 2, 2, 2, 2), (5, 5, 5, 5, 5, 5, 5, 5), (2, 2, 2, 2, 2, 2, 2, 2)]
PROGRAM = [
    ("piece", 0, 4),
    ("piece", 2, 0),
    ("piece", 3, 0),
    ("piece", 0, 5),
    ("piece", 2, 3),
    ("piece", 3, 3),
    ("piece", 0, 6),
    ("piece", 2, 2),
    ("piece", 3, 2),
    ("piece", 0, 7),
    ("piece", 2, 1),
    ("piece", 3, 1),
    ("piece", 6, 0),
    ("piece", 8, 0),
    ("piece", 2, 4),
    ("piece", 4, 0),
    ("piece", 6, 3),
    ("piece", 8, 3),
    ("piece", 2, 5),
    ("piece", 4, 3),
    ("piece", 6, 2),
    ("piece", 8, 2),
    ("piece", 2, 6),
    ("piece", 3, 6),
    ("twin", 0, 0),
    ("twin", 0, 1),
    ("products", ((0, 0, False),)),
    ("piece", 6, 1),
    ("piece", 8, 1),
    ("piece", 2, 7),
    ("piece", 4, 2),
    ("products", ((2, 0, True),)),
    ("piece", 6, 4),
    ("piece", 8, 4),
    ("piece", 4, 1),
    ("piece", 5, 0),
    ("piece", 6, 5),
    ("piece", 8, 5),
    ("piece", 3, 4),
    ("piece", 5, 3),
    ("piece", 6, 6),
    ("piece", 8, 6),
    ("piece", 4, 6),
    ("piece", 5, 2),
    ("piece", 6, 7),
    ("piece", 8, 7),
    ("products", ((6, 0, True),)),
    ("piece", 3, 5),
    ("piece", 5, 1),
    ("twin", 2, 0),
    ("twin", 2, 1),
    ("products", ((6, 2, True),)),
    ("piece", 1, 0),
    ("piece", 7, 0),
    ("known",),
    ("piece", 3, 7),
    ("piece", 5, 4),
    ("products", ((8, 0, True),)),
    ("piece", 1, 3),
    ("piece", 7, 3),
    ("products", ((3, 2, True),)),
    ("piece", 4, 4),
    ("piece", 5, 5),
    ("piece", 1, 2),
    ("piece", 7, 2),
    ("twin", 8, 0),
    ("twin", 8, 1),
    ("products", ((3, 8, True),)),
    ("piece", 5, 6),
    ("products", ((6, 8, False),)),
    ("piece", 1, 1),
    ("piece", 4, 5),
    ("piece", 7, 1),
    ("piece", 5, 7),
    ("twin", 3, 0),
    ("twin", 3, 1),
    ("products", ((6, 3, True),)),
    ("piece", 1, 4),
    ("piece", 4, 7),
    ("piece", 7, 4),
    ("products", ((5, 3, True), (5, 8, True))),
    ("piece", 1, 5),
    ("piece", 7, 5),
    ("products", ((4, 2, True), (4, 8, True))),
    ("piece", 1, 6),
    ("piece", 7, 6),
    ("twin", 5, 0),
    ("twin", 5, 1),
    ("products", ((4, 5, True),)),
    ("piece", 1, 7),
    ("piece", 7, 7),
    ("twin", 4, 0),
    ("twin", 4, 1),
    ("products", ((1, 4, False), (7, 0, True), (7, 3, True), (7, 4, False))),
]
D = 768
MEM = 256
BLOCKS = 64
PIECES = len(ROUTE[0])
HALF = PIECES // 2
ROWS = MEM // PIECES
NEVER = float(1 << 20)
MESH = pl.DeviceIdType.MESH
FAR_FIRST = (4, 3, 5, 2, 6, 1, 7, 0)
F32 = jnp.float32
N_SLOTS = len(AT)
PRODUCTS = [one for step in PROGRAM if step[0] == "products" for one in step[1]]
LEFT = sorted({one[0] for one in PRODUCTS})
RIGHT = sorted({one[1] for one in PRODUCTS})
BASE = [s + sum(r < s for r in RIGHT) for s in range(N_SLOTS)]
N_HELD = N_SLOTS + len(RIGHT)
PARTS = [(AT[s], 0) for s in LEFT] + [(AT[s], other) for s in RIGHT for other in (0, 1)]
STEPS = {tuple((a - b) for a, b in zip(AT[s], AT[ROUTE[s - 1][q]])) for s in range(1, N_SLOTS) for q in range(PIECES)}
N_SENT = PIECES * (N_SLOTS - 1) + PIECES * len(RIGHT) + HALF


def coordinates():
    store = lax.axis_index("store")
    return store // 16, (store // 8) % 2, store % 8, lax.axis_index("grid"), lax.axis_index("row")


def device(x, y_hi, z, core, y_lo):
    return (x * 16 + y_hi * 8 + z, core, y_lo)


def spread(row):
    return jnp.transpose(jnp.broadcast_to(row, (128, 128)))


def lookup(n, values):
    if len(set(values)) == 1:
        return values[0]
    found = jnp.int32(values[0])
    for k in range(1, len(values)):
        if values[k] != values[0]:
            found = jnp.where(n == k, jnp.int32(values[k]), found)
    return found


def kernel(emb_hbm, members_hbm, order_hbm, sizes_hbm, out, sizes, emb, members, order, table, held, give, vec, col_ord, row_ord, col_best, row_best, lines, tell, got, swap, load_sem, send_sem, recv_sem, twin_sem, route_send, route_recv, known):
    x, y_hi, z, core, y_lo = coordinates()
    y = y_hi * 2 + y_lo
    store = x * 16 + y_hi * 8 + z

    def at(dx, dz, other=0, across=False):
        side = core if other == 0 else 1 - core
        if across:
            return device((x + dx + 4) % 4, 1 - y_hi, (z + dz + 8) % 8, side, 1 - y_lo)
        return device((x + dx + 4) % 4, y_hi, (z + dz + 8) % 8, side, y_lo)

    near = sorted({((sign * dx) % 4, (sign * dz) % 8) for dx, dz in STEPS for sign in (1, -1)})
    greet = [at(dx, dz) for dx, dz in near] + [at(0, 0, 0, True), at(0, 0, 1)]
    greet += [device(x, y_hi, z, core, 1 - y_lo), device(x, 1 - y_hi, z, core, y_lo)]
    barrier = pltpu.get_barrier_semaphore()
    for one in greet:
        pl.semaphore_signal(barrier, inc=1, device_id=one, device_id_type=MESH)

    loads = [
        pltpu.make_async_copy(members_hbm, members, load_sem.at[0]),
        pltpu.make_async_copy(order_hbm, order, load_sem.at[1]),
        pltpu.make_async_copy(emb_hbm, emb, load_sem.at[2]),
        pltpu.make_async_copy(sizes_hbm, sizes, load_sem.at[3]),
    ]
    for one in loads:
        one.start()
    loads[0].wait()

    def lay(ref, cluster, where):
        for b in range(BLOCKS):
            line = ref[pl.ds(cluster, 1), b * MEM : (b + 1) * MEM]
            table[where, b : b + 1, :] = line
            table[where, BLOCKS + b : BLOCKS + b + 1, :] = line

    lay(members, y, 0)
    lay(members, 3 - y, 1)
    ids = jnp.transpose(table[0])
    ids_partner = jnp.transpose(table[1])
    upper = lax.broadcasted_iota(jnp.int32, (1, 128), 1) // BLOCKS
    before = (
        lax.broadcasted_iota(jnp.int32, (MEM, MEM), 1) < lax.broadcasted_iota(jnp.int32, (MEM, MEM), 0)
    ).astype(jnp.bfloat16)

    def ranks(local):
        inside = (local >= 0) & (local < 2048)
        count = jnp.dot(before, jnp.where(inside, 1.0, 0.0).astype(jnp.bfloat16), preferred_element_type=F32)
        return jnp.where(inside, count, -1.0)

    def pick(rank, side, values):
        wanted = (2 * side + upper).astype(F32)
        return jnp.sum(jnp.where(rank == wanted, values, 0.0), axis=0, keepdims=True)

    chosen = []
    for table_ids in (ids_partner, ids):
        local = table_ids - store * 2048
        chosen.append(spread(pick(ranks(local), core, local.astype(F32))).astype(jnp.int32))
    loads[2].wait()
    lane = lax.broadcasted_iota(jnp.int32, (128, 128), 1)
    for half in range(2):
        onehot = jnp.concatenate([jnp.where(chosen[half] == lane + 128 * j, 1.0, 0.0).astype(jnp.bfloat16) for j in range(16)], axis=1)
        for n in range(3):
            vec[:, n * 256 : (n + 1) * 256] = jnp.dot(onehot, emb[:, n * 256 : (n + 1) * 256], preferred_element_type=F32)
        vector = vec[...]
        scale = lax.rsqrt(jnp.sum(vector * vector, axis=1, keepdims=True) + 1e-06)
        unit = (vector * scale).astype(jnp.bfloat16).reshape(HALF, ROWS, D)
        if half == 0:
            give[...] = unit
        else:
            held[pl.ds(y_hi * HALF, HALF)] = unit

    pl.semaphore_wait(barrier, len(greet))

    def side_of(half):
        return y_hi if half == 0 else 1 - y_hi

    def piece(slot, q):
        return BASE[slot] * PIECES + side_of(q // HALF) * HALF + q % HALF

    def push(src, dst, sem, to):
        pltpu.make_async_remote_copy(src, dst, send_sem.at[0], sem, device_id=to, device_id_type=MESH).start()

    def landed(ref, sem):
        pltpu.make_async_remote_copy(ref, ref, send_sem.at[0], sem, device_id=at(0, 0, 1), device_id_type=MESH).wait_recv()

    def forward(slot, q):
        for s in range(1, N_SLOTS):
            if ROUTE[s - 1][q] == slot:
                push(held.at[piece(slot, q)], held.at[piece(s, q)], recv_sem.at[s * PIECES + q], at(AT[slot][0] - AT[s][0], AT[slot][1] - AT[s][1]))

    def twin(slot, half):
        if slot in RIGHT:
            where = BASE[slot] * PIECES + side_of(half) * HALF
            push(held.at[pl.ds(where, HALF)], held.at[pl.ds(where + PIECES, HALF)], twin_sem.at[slot * 2 + half], at(0, 0, 1))

    for q in range(HALF):
        push(give.at[q], held.at[y_hi * HALF + q], recv_sem.at[HALF + q], at(0, 0, 0, True))
        forward(0, q)
    twin(0, 0)

    loads[1].wait()
    loads[3].wait()
    lay(order, y, 2)
    slot = lax.broadcasted_iota(jnp.int32, (MEM, 128), 0) + MEM * (lax.broadcasted_iota(jnp.int32, (MEM, 128), 1) % BLOCKS)
    rank_of = jnp.where(slot < sizes[y], jnp.transpose(table[2]).astype(F32), NEVER)
    for s in range(N_SLOTS):
        for hi in range(2):
            shard = ((x + AT[s][0] + 4) % 4) * 16 + hi * 8 + (z + AT[s][1] + 8) % 8
            rank = ranks(ids - shard * 2048)
            line = pick(rank, core, rank_of)
            if s in LEFT:
                row_ord[LEFT.index(s), hi * 128 : (hi + 1) * 128, :] = spread(line)
            if s in RIGHT:
                r = RIGHT.index(s)
                col_ord[r, :, hi * 128 : (hi + 1) * 128] = jnp.broadcast_to(line, (8, 128))
                line = pick(rank, 1 - core, rank_of)
                col_ord[r, :, 256 + hi * 128 : 256 + (hi + 1) * 128] = jnp.broadcast_to(line, (8, 128))
    col_best[...] = jnp.full(col_best.shape, -1.0, F32)
    row_best[...] = jnp.full(row_best.shape, -1.0, F32)

    def products(group):
        def one(n, carry):
            left = lookup(n, [LEFT.index(a) for a, b, full in group])
            left_at = lookup(n, [BASE[a] * PIECES for a, b, full in group])
            right = lookup(n, [RIGHT.index(b) for a, b, full in group])
            right_at = lookup(n, [BASE[b] * PIECES for a, b, full in group])
            column = lookup(n, [RIGHT.index(b) if full else len(RIGHT) for a, b, full in group])
            a = held[pl.ds(left_at, PIECES)].reshape(MEM, D)
            b = held[pl.ds(right_at, 2 * PIECES)].reshape(2 * MEM, D)
            score = lax.dot_general(a, b, (((1,), (1,)), ((), ())), preferred_element_type=F32)
            own = row_ord[left]
            best = row_best[left]
            for part in range(4):
                lanes = slice(part * 128, (part + 1) * 128)
                mine = score[:, lanes]
                earlier = col_ord[right, 0:1, lanes] < own
                best = jnp.maximum(best, jnp.where(earlier, mine, -1.0))
                later = jnp.max(jnp.where(earlier, -1.0, mine).reshape(32, 8, 128), axis=0)
                col_best[column, :, lanes] = jnp.maximum(col_best[column, :, lanes], later)
            row_best[left] = best
            return carry

        if len(group) == 1:
            one(0, 0)
        else:
            lax.fori_loop(0, len(group), one, 0, unroll=True)

    for step in PROGRAM:
        if step[0] == "piece":
            s, q = step[1:]
            landed(held.at[piece(s, q)], recv_sem.at[s * PIECES + q])
            forward(s, q)
            half = {("piece", s, r) for r in range(PIECES) if r // HALF == q // HALF}
            if half <= set(PROGRAM[: PROGRAM.index(step) + 1]):
                twin(s, q // HALF)
        elif step[0] == "known":
            for s in range(N_SLOTS):
                for other in (0, 1):
                    if s > 0 or other > 0:
                        pl.semaphore_signal(known, inc=1, device_id=at(AT[s][0], AT[s][1], other), device_id_type=MESH)
        elif step[0] == "twin":
            s, half = step[1:]
            landed(held.at[pl.ds(BASE[s] * PIECES + PIECES + side_of(half) * HALF, HALF)], twin_sem.at[s * 2 + half])
        else:
            products(step[1])

    for p in range(len(PARTS)):
        for hi in range(2):
            if p < len(LEFT):
                line = jnp.max(jnp.transpose(row_best[p, hi * 128 : (hi + 1) * 128, :]), axis=0, keepdims=True)
            else:
                r, other = (p - len(LEFT)) // 2, (p - len(LEFT)) % 2
                line = jnp.max(col_best[r, :, other * 256 + hi * 128 : other * 256 + (hi + 1) * 128], axis=0, keepdims=True)
            lines[p * 2 + hi : p * 2 + hi + 1, :] = line
    turned = jnp.transpose(lines[...])
    tell[:, 0, :] = turned[:BLOCKS]
    tell[:, 1, :] = turned[BLOCKS:]

    pl.semaphore_wait(known, 2 * N_SLOTS - 1)

    sender = (x * 8 + z) * 2 + core
    home = (y_hi * 8 + z) * 4 + core * 2 + y_lo

    def route(n, carry):
        to_z = lax.rem(z + lookup(n, FAR_FIRST), 8)
        for over, low in ((1, 0), (1, 1), (0, 1), (0, 0)):
            to_hi = 1 - y_hi if over else y_hi
            to_lo = 1 - y_lo if low else y_lo
            for twin_core in (1, 0):
                to_core = 1 - core if twin_core else core
                store_there = to_hi * 8 + to_z

                def remote():
                    pltpu.make_async_remote_copy(
                        tell.at[store_there * 4 + to_core * 2 + to_lo],
                        got.at[sender],
                        route_send.at[0],
                        route_recv.at[0],
                        device_id=(y * 16 + store_there, to_core, to_lo),
                        device_id_type=MESH,
                    ).start()

                if over or low or twin_core:
                    remote()
                else:
                    here = (x == y) & (n == len(FAR_FIRST) - 1)
                    pl.when(jnp.logical_not(here))(remote)

                    @pl.when(here)
                    def _():
                        pltpu.make_async_copy(tell.at[home], got.at[sender], route_recv.at[0]).start()

        return carry

    lax.fori_loop(0, len(FAR_FIRST), route, 0)

    block = home
    own_ids = members[pl.ds(x, 1), pl.ds(pl.multiple_of(block * MEM, MEM), MEM)]
    shard = own_ids // 2048
    shard_rows = jnp.concatenate([spread(shard[:, :128].astype(F32)), spread(shard[:, 128:].astype(F32))], axis=0)
    shard_rows = jnp.concatenate([shard_rows, shard_rows], axis=1)
    same = (shard_rows == shard.astype(F32)) & (
        lax.broadcasted_iota(jnp.int32, (MEM, MEM), 0) < lax.broadcasted_iota(jnp.int32, (MEM, MEM), 1)
    )
    rank = jnp.sum(jnp.where(same, 1.0, 0.0), axis=0, keepdims=True).astype(jnp.int32)
    from_sender = ((shard // 16) * 8 + shard % 8) * 2 + rank // 2
    from_place = (rank % 2) * 2 + (shard // 8) % 2
    from_which = from_sender * 4 + from_place
    slots = block * MEM + lax.broadcasted_iota(jnp.int32, (1, MEM), 1)
    in_use = slots < sizes[x]
    lane_z = lax.broadcasted_iota(jnp.int32, (4, 128), 1) % 16
    senders = lax.broadcasted_iota(jnp.int32, (64, MEM), 0)

    pltpu.make_async_remote_copy(got, got, route_send.at[0], route_recv.at[0], device_id=at(0, 0, 1), device_id_type=MESH).wait_recv()
    for rr in range(2):
        heard = got[:, rr, :]
        swap[rr] = jnp.transpose(jnp.concatenate([heard, heard], axis=0))
    value = jnp.full((4, 128), -1.0, F32)
    for p in range(len(PARTS)):
        (dx, dz), other = PARTS[p]
        rows = jnp.concatenate([swap[0, 2 * p : 2 * p + 2, :], swap[1, 2 * p : 2 * p + 2, :]], axis=0)
        if dx % 4 or dz % 8:
            turn = 16 * (dx % 4) + 2 * (dz % 8)
            moved = pltpu.roll(rows, turn, 1)
            if dz % 8:
                moved = jnp.where(lane_z >= 2 * (dz % 8), moved, pltpu.roll(rows, (turn - 16) % 128, 1))
            rows = moved
        if other:
            rows = jnp.where(lane_z % 2 == 0, pltpu.roll(rows, 127, 1), pltpu.roll(rows, 1, 1))
        value = jnp.maximum(value, rows)
    final = jnp.zeros((1, MEM), F32)
    for place in range(4):
        column = spread(value[place : place + 1, :])[:64]
        column = jnp.concatenate([column, column], axis=1)
        here = from_which == senders * 4 + place
        final = final + jnp.sum(jnp.where(here, column, 0.0), axis=0, keepdims=True)
    out[...] = jnp.where(in_use, final, 0.0)

    sent = held.at[pl.ds(0, N_SENT)]
    pltpu.make_async_remote_copy(sent, sent, send_sem.at[0], recv_sem.at[0], device_id=at(0, 0, 1), device_id_type=MESH).wait_send()

    @pl.when(x == y)
    def _():
        fewer = got.at[pl.ds(0, 63)]
        pltpu.make_async_remote_copy(fewer, fewer, route_send.at[0], route_recv.at[0], device_id=at(0, 0, 1), device_id_type=MESH).wait_send()

    @pl.when(x != y)
    def _():
        pltpu.make_async_remote_copy(got, got, route_send.at[0], route_recv.at[0], device_id=at(0, 0, 1), device_id_type=MESH).wait_send()


def on_device(embeddings, members, order, sizes):
    vmem = pltpu.VMEM
    dma = pltpu.SemaphoreType.DMA
    best = pl.pallas_call(
        kernel,
        out_shape=jax.ShapeDtypeStruct((1, MEM), F32),
        in_specs=[pl.BlockSpec(memory_space=pltpu.HBM)] * 4,
        out_specs=pl.BlockSpec(memory_space=pltpu.VMEM),
        scratch_shapes=[
            pltpu.SMEM((4,), jnp.int32),
            vmem((2048, D), jnp.bfloat16),
            vmem((4, 16384), jnp.int32),
            vmem((4, 16384), jnp.int32),
            vmem((3, 128, MEM), jnp.int32),
            vmem((max(N_HELD * PIECES, N_SENT), ROWS, D), jnp.bfloat16),
            vmem((HALF, ROWS, D), jnp.bfloat16),
            vmem((128, D), F32),
            vmem((len(RIGHT), 8, 512), F32),
            vmem((len(LEFT), MEM, 128), F32),
            vmem((len(RIGHT) + 1, 8, 512), F32),
            vmem((len(LEFT), MEM, 128), F32),
            vmem((128, 128), F32),
            vmem((64, 2, 128), F32),
            vmem((64, 2, 128), F32),
            vmem((2, 128, 128), F32),
            dma((4,)),
            dma((1,)),
            dma((N_SLOTS * PIECES,)),
            dma((N_SLOTS * 2,)),
            dma((1,)),
            dma((1,)),
            pltpu.SemaphoreType.REGULAR,
        ],
        compiler_params=pltpu.CompilerParams(collective_id=0, has_side_effects=True, vmem_limit_bytes=48 << 20),
        cost_estimate=pl.CostEstimate(flops=8 << 30, bytes_accessed=8 << 20, transcendentals=0),
    )(*[pltpu.with_memory_space_constraint(one, pltpu.HBM) for one in (embeddings, members, order, sizes)])
    return best.reshape(MEM)


def solution(mesh):
    return jax.shard_map(
        on_device,
        mesh=mesh,
        in_specs=(P("store", None), P(), P(), P()),
        out_specs=P(("store", "grid", "row")),
        check_vma=False,
    )
```

```python
import jax
import jax.numpy as jnp
from jax import lax
from jax.experimental import pallas as pl
from jax.experimental.pallas import tpu as pltpu
from jax.sharding import PartitionSpec as P

AT = [(0, 0), (0, -2), (0, -1), (0, 1), (0, 2), (1, 1), (2, 2), (-1, 1), (-1, 2)]
ROUTE = [(2, 2, 2, 2, 2, 2, 2, 2), (0, 0, 0, 0, 0, 0, 0, 0), (0, 0, 0, 0, 0, 0, 0, 0), (8, 8, 8, 8, 8, 8, 3, 8), (3, 3, 3, 3, 3, 3, 3, 3), (8, 8, 8, 8, 8, 8, 8, 8), (3, 3, 3, 3, 3, 3, 3, 3), (7, 7, 7, 7, 7, 7, 7, 7)]
PROGRAM = [
    ("send", 2, 1),
    ("send", 3, 1),
    ("send", 2, 3),
    ("send", 3, 3),
    ("send", 2, 0),
    ("send", 3, 0),
    ("send", 2, 2),
    ("send", 3, 2),
    ("piece", 0, 4),
    ("piece", 2, 1),
    ("piece", 3, 1),
    ("send", 1, 1),
    ("send", 3, 4),
    ("send", 5, 1),
    ("send", 7, 1),
    ("send", 2, 4),
    ("piece", 0, 5),
    ("piece", 2, 3),
    ("piece", 3, 3),
    ("send", 1, 3),
    ("send", 3, 5),
    ("send", 5, 3),
    ("send", 7, 3),
    ("piece", 0, 6),
    ("piece", 2, 0),
    ("piece", 3, 0),
    ("send", 3, 6),
    ("send", 5, 0),
    ("send", 7, 0),
    ("piece", 0, 7),
    ("piece", 2, 2),
    ("piece", 3, 2),
    ("send", 2, 7),
    ("send", 3, 7),
    ("send", 5, 2),
    ("send", 7, 2),
    ("send", 2, 5),
    ("piece", 5, 1),
    ("piece", 7, 1),
    ("send", 8, 1),
    ("piece", 1, 1),
    ("piece", 3, 4),
    ("send", 5, 4),
    ("send", 7, 4),
    ("piece", 5, 3),
    ("piece", 7, 3),
    ("send", 8, 3),
    ("piece", 2, 4),
    ("piece", 3, 5),
    ("send", 1, 4),
    ("send", 5, 5),
    ("send", 7, 5),
    ("send", 1, 0),
    ("piece", 5, 0),
    ("piece", 7, 0),
    ("send", 8, 0),
    ("twin", 0, 0),
    ("twin", 0, 1),
    ("products", ((0, 0, False),)),
    ("piece", 1, 3),
    ("piece", 3, 6),
    ("send", 5, 6),
    ("send", 7, 6),
    ("piece", 5, 2),
    ("piece", 7, 2),
    ("piece", 2, 7),
    ("piece", 3, 7),
    ("send", 1, 7),
    ("send", 5, 7),
    ("send", 7, 7),
    ("send", 2, 6),
    ("piece", 5, 4),
    ("piece", 7, 4),
    ("send", 8, 4),
    ("send", 8, 2),
    ("products", ((3, 0, True),)),
    ("send", 1, 2),
    ("piece", 2, 5),
    ("piece", 8, 1),
    ("send", 4, 1),
    ("send", 6, 1),
    ("piece", 5, 5),
    ("piece", 7, 5),
    ("send", 8, 5),
    ("send", 1, 5),
    ("piece", 1, 4),
    ("piece", 8, 3),
    ("send", 4, 3),
    ("send", 6, 3),
    ("piece", 5, 6),
    ("piece", 7, 6),
    ("piece", 1, 0),
    ("piece", 8, 0),
    ("send", 4, 0),
    ("send", 6, 0),
    ("piece", 5, 7),
    ("piece", 7, 7),
    ("send", 8, 7),
    ("send", 8, 6),
    ("products", ((5, 0, True),)),
    ("send", 4, 6),
    ("piece", 1, 7),
    ("piece", 8, 4),
    ("send", 4, 4),
    ("send", 6, 4),
    ("piece", 4, 1),
    ("piece", 6, 1),
    ("known",),
    ("products", ((7, 0, True),)),
    ("piece", 2, 6),
    ("piece", 8, 2),
    ("send", 1, 6),
    ("send", 4, 2),
    ("send", 6, 2),
    ("piece", 4, 3),
    ("piece", 6, 3),
    ("twin", 5, 0),
    ("twin", 5, 1),
    ("products", ((2, 5, True),)),
    ("piece", 1, 2),
    ("piece", 8, 5),
    ("send", 4, 5),
    ("send", 6, 5),
    ("piece", 4, 0),
    ("piece", 6, 0),
    ("products", ((3, 5, True), (7, 5, False))),
    ("piece", 1, 5),
    ("piece", 8, 7),
    ("send", 4, 7),
    ("send", 6, 7),
    ("piece", 4, 4),
    ("piece", 6, 4),
    ("twin", 2, 0),
    ("twin", 2, 1),
    ("products", ((3, 2, True), (7, 2, True))),
    ("piece", 8, 6),
    ("send", 6, 6),
    ("piece", 1, 6),
    ("piece", 4, 2),
    ("piece", 6, 2),
    ("products", ((8, 2, True), (8, 5, True))),
    ("piece", 4, 6),
    ("piece", 4, 5),
    ("piece", 6, 5),
    ("products", ((1, 5, True),)),
    ("piece", 4, 7),
    ("piece", 6, 7),
    ("products", ((4, 2, True),)),
    ("twin", 1, 0),
    ("twin", 1, 1),
    ("products", ((4, 1, False),)),
    ("piece", 6, 6),
    ("products", ((8, 1, True), (6, 0, True), (6, 1, False), (6, 2, True))),
]
D = 768
MEM = 256
BLOCKS = 64
PIECES = len(ROUTE[0])
HALF = PIECES // 2
ROWS = MEM // PIECES
NEVER = float(1 << 20)
MESH = pl.DeviceIdType.MESH
FAR_FIRST = (4, 3, 5, 2, 6, 1, 7, 0)
F32 = jnp.float32
N_SLOTS = len(AT)
PRODUCTS = [one for step in PROGRAM if step[0] == "products" for one in step[1]]
LEFT = sorted({one[0] for one in PRODUCTS})
RIGHT = sorted({one[1] for one in PRODUCTS})
BASE = [s + sum(r < s for r in RIGHT) for s in range(N_SLOTS)]
N_HELD = N_SLOTS + len(RIGHT)
PARTS = [(AT[s], 0) for s in LEFT] + [(AT[s], other) for s in RIGHT for other in (0, 1)]
STEPS = {tuple((a - b) for a, b in zip(AT[s], AT[ROUTE[s - 1][q]])) for s in range(1, N_SLOTS) for q in range(PIECES)}
N_SENT = PIECES * (N_SLOTS - 1) + PIECES * len(RIGHT) + HALF


def coordinates():
    store = lax.axis_index("store")
    return store // 16, (store // 8) % 2, store % 8, lax.axis_index("grid"), lax.axis_index("row")


def device(x, y_hi, z, core, y_lo):
    return (x * 16 + y_hi * 8 + z, core, y_lo)


def spread(row):
    return jnp.transpose(jnp.broadcast_to(row, (128, 128)))


def lookup(n, values):
    if len(set(values)) == 1:
        return values[0]
    found = jnp.int32(values[0])
    for k in range(1, len(values)):
        if values[k] != values[0]:
            found = jnp.where(n == k, jnp.int32(values[k]), found)
    return found


def kernel(emb_hbm, members_hbm, order_hbm, sizes_hbm, out, sizes, emb, members, order, table, held, give, vec, col_ord, row_ord, col_best, row_best, lines, tell, got, swap, load_sem, send_sem, recv_sem, twin_sem, route_send, route_recv, known):
    x, y_hi, z, core, y_lo = coordinates()
    y = y_hi * 2 + y_lo
    store = x * 16 + y_hi * 8 + z

    def at(dx, dz, other=0, across=False):
        side = core if other == 0 else 1 - core
        if across:
            return device((x + dx + 4) % 4, 1 - y_hi, (z + dz + 8) % 8, side, 1 - y_lo)
        return device((x + dx + 4) % 4, y_hi, (z + dz + 8) % 8, side, y_lo)

    near = sorted({((sign * dx) % 4, (sign * dz) % 8) for dx, dz in STEPS for sign in (1, -1)})
    greet = [at(dx, dz) for dx, dz in near] + [at(0, 0, 0, True), at(0, 0, 1)]
    greet += [device(x, y_hi, z, side, 1 - y_lo) for side in (core, 1 - core)]
    greet += [device(x, 1 - y_hi, z, side, y_lo) for side in (core, 1 - core)]
    greet.append(device(x, 1 - y_hi, z, 1 - core, 1 - y_lo))
    barrier = pltpu.get_barrier_semaphore()
    for one in greet:
        pl.semaphore_signal(barrier, inc=1, device_id=one, device_id_type=MESH)

    loads = [
        pltpu.make_async_copy(members_hbm, members, load_sem.at[0]),
        pltpu.make_async_copy(order_hbm, order, load_sem.at[1]),
        pltpu.make_async_copy(emb_hbm, emb, load_sem.at[2]),
        pltpu.make_async_copy(sizes_hbm, sizes, load_sem.at[3]),
    ]
    for one in loads:
        one.start()
    loads[0].wait()

    def lay(ref, cluster, where):
        for b in range(BLOCKS):
            line = ref[pl.ds(cluster, 1), b * MEM : (b + 1) * MEM]
            table[where, b : b + 1, :] = line
            table[where, BLOCKS + b : BLOCKS + b + 1, :] = line

    lay(members, y, 0)
    lay(members, 3 - y, 1)
    ids = jnp.transpose(table[0])
    ids_partner = jnp.transpose(table[1])
    upper = lax.broadcasted_iota(jnp.int32, (1, 128), 1) // BLOCKS
    before = (
        lax.broadcasted_iota(jnp.int32, (MEM, MEM), 1) < lax.broadcasted_iota(jnp.int32, (MEM, MEM), 0)
    ).astype(jnp.bfloat16)

    def ranks(local):
        inside = (local >= 0) & (local < 2048)
        count = jnp.dot(before, jnp.where(inside, 1.0, 0.0).astype(jnp.bfloat16), preferred_element_type=F32)
        return jnp.where(inside, count, -1.0)

    def pick(rank, side, values):
        wanted = (2 * side + upper).astype(F32)
        return jnp.sum(jnp.where(rank == wanted, values, 0.0), axis=0, keepdims=True)

    chosen = []
    for table_ids in (ids_partner, ids):
        local = table_ids - store * 2048
        chosen.append(spread(pick(ranks(local), core, local.astype(F32))).astype(jnp.int32))
    loads[2].wait()
    lane = lax.broadcasted_iota(jnp.int32, (128, 128), 1)
    for half in range(2):
        onehot = jnp.concatenate([jnp.where(chosen[half] == lane + 128 * j, 1.0, 0.0).astype(jnp.bfloat16) for j in range(16)], axis=1)
        for n in range(3):
            vec[:, n * 256 : (n + 1) * 256] = jnp.dot(onehot, emb[:, n * 256 : (n + 1) * 256], preferred_element_type=F32)
        vector = vec[...]
        scale = lax.rsqrt(jnp.sum(vector * vector, axis=1, keepdims=True) + 1e-06)
        unit = (vector * scale).astype(jnp.bfloat16).reshape(HALF, ROWS, D)
        if half == 0:
            give[...] = unit
        else:
            held[pl.ds(y_hi * HALF, HALF)] = unit

    pl.semaphore_wait(barrier, len(greet))

    def side_of(half):
        return y_hi if half == 0 else 1 - y_hi

    def piece(slot, q):
        return BASE[slot] * PIECES + side_of(q // HALF) * HALF + q % HALF

    def push(src, dst, sem, to):
        pltpu.make_async_remote_copy(src, dst, send_sem.at[0], sem, device_id=to, device_id_type=MESH).start()

    def landed(ref, sem):
        pltpu.make_async_remote_copy(ref, ref, send_sem.at[0], sem, device_id=at(0, 0, 1), device_id_type=MESH).wait_recv()

    def send(s, q):
        slot = ROUTE[s - 1][q]
        push(held.at[piece(slot, q)], held.at[piece(s, q)], recv_sem.at[s * PIECES + q], at(AT[slot][0] - AT[s][0], AT[slot][1] - AT[s][1]))

    def twin(slot, half):
        if slot in RIGHT:
            where = BASE[slot] * PIECES + side_of(half) * HALF
            push(held.at[pl.ds(where, HALF)], held.at[pl.ds(where + PIECES, HALF)], twin_sem.at[slot * 2 + half], at(0, 0, 1))

    for q in range(HALF):
        push(give.at[q], held.at[y_hi * HALF + q], recv_sem.at[HALF + q], at(0, 0, 0, True))
    first = [step[0] for step in PROGRAM].index("piece")
    for step in PROGRAM[:first]:
        send(*step[1:])
    twin(0, 0)

    loads[1].wait()
    loads[3].wait()
    lay(order, y, 2)
    slot = lax.broadcasted_iota(jnp.int32, (MEM, 128), 0) + MEM * (lax.broadcasted_iota(jnp.int32, (MEM, 128), 1) % BLOCKS)
    rank_of = jnp.where(slot < sizes[y], jnp.transpose(table[2]).astype(F32), NEVER)
    for s in range(N_SLOTS):
        for hi in range(2):
            shard = ((x + AT[s][0] + 4) % 4) * 16 + hi * 8 + (z + AT[s][1] + 8) % 8
            rank = ranks(ids - shard * 2048)
            line = pick(rank, core, rank_of)
            if s in LEFT:
                row_ord[LEFT.index(s), hi * 128 : (hi + 1) * 128, :] = spread(line)
            if s in RIGHT:
                r = RIGHT.index(s)
                col_ord[r, :, hi * 128 : (hi + 1) * 128] = jnp.broadcast_to(line, (8, 128))
                line = pick(rank, 1 - core, rank_of)
                col_ord[r, :, 256 + hi * 128 : 256 + (hi + 1) * 128] = jnp.broadcast_to(line, (8, 128))
    col_best[...] = jnp.full(col_best.shape, -1.0, F32)
    row_best[...] = jnp.full(row_best.shape, -1.0, F32)

    def products(group):
        def one(n, carry):
            left = lookup(n, [LEFT.index(a) for a, b, full in group])
            left_at = lookup(n, [BASE[a] * PIECES for a, b, full in group])
            right = lookup(n, [RIGHT.index(b) for a, b, full in group])
            right_at = lookup(n, [BASE[b] * PIECES for a, b, full in group])
            column = lookup(n, [RIGHT.index(b) if full else len(RIGHT) for a, b, full in group])
            a = held[pl.ds(left_at, PIECES)].reshape(MEM, D)
            b = held[pl.ds(right_at, 2 * PIECES)].reshape(2 * MEM, D)
            score = lax.dot_general(a, b, (((1,), (1,)), ((), ())), preferred_element_type=F32)
            own = row_ord[left]
            best = row_best[left]
            for part in range(4):
                lanes = slice(part * 128, (part + 1) * 128)
                mine = score[:, lanes]
                earlier = col_ord[right, 0:1, lanes] < own
                best = jnp.maximum(best, jnp.where(earlier, mine, -1.0))
                later = jnp.max(jnp.where(earlier, -1.0, mine).reshape(32, 8, 128), axis=0)
                col_best[column, :, lanes] = jnp.maximum(col_best[column, :, lanes], later)
            row_best[left] = best
            return carry

        if len(group) == 1:
            one(0, 0)
        else:
            lax.fori_loop(0, len(group), one, 0, unroll=True)

    for step in PROGRAM[first:]:
        if step[0] == "send":
            send(*step[1:])
        elif step[0] == "piece":
            s, q = step[1:]
            landed(held.at[piece(s, q)], recv_sem.at[s * PIECES + q])
            half = {("piece", s, r) for r in range(PIECES) if r // HALF == q // HALF}
            if half <= set(PROGRAM[: PROGRAM.index(step) + 1]):
                twin(s, q // HALF)
        elif step[0] == "known":
            for s in range(1, N_SLOTS):
                pl.semaphore_signal(known, inc=1, device_id=at(AT[s][0], AT[s][1]), device_id_type=MESH)
        elif step[0] == "twin":
            s, half = step[1:]
            landed(held.at[pl.ds(BASE[s] * PIECES + PIECES + side_of(half) * HALF, HALF)], twin_sem.at[s * 2 + half])
        else:
            products(step[1])

    for p in range(len(PARTS)):
        for hi in range(2):
            if p < len(LEFT):
                line = jnp.max(jnp.transpose(row_best[p, hi * 128 : (hi + 1) * 128, :]), axis=0, keepdims=True)
            else:
                r, other = (p - len(LEFT)) // 2, (p - len(LEFT)) % 2
                line = jnp.max(col_best[r, :, other * 256 + hi * 128 : other * 256 + (hi + 1) * 128], axis=0, keepdims=True)
            lines[p * 2 + hi : p * 2 + hi + 1, :] = line
    turned = jnp.transpose(lines[...])
    tell[:, 0, :] = turned[:BLOCKS]
    tell[:, 1, :] = turned[BLOCKS:]

    pl.semaphore_wait(known, N_SLOTS - 1)

    sender = (x * 8 + z) * 2 + core
    home = (y_hi * 8 + z) * 4 + core * 2 + y_lo

    def route(n, carry):
        to_z = lax.rem(z + lookup(n, FAR_FIRST), 8)
        for over, low in ((1, 0), (1, 1), (0, 1), (0, 0)):
            to_hi = 1 - y_hi if over else y_hi
            to_lo = 1 - y_lo if low else y_lo
            for twin_core in (1, 0):
                to_core = 1 - core if twin_core else core
                store_there = to_hi * 8 + to_z

                def remote():
                    pltpu.make_async_remote_copy(
                        tell.at[store_there * 4 + to_core * 2 + to_lo],
                        got.at[sender],
                        route_send.at[0],
                        route_recv.at[0],
                        device_id=(y * 16 + store_there, to_core, to_lo),
                        device_id_type=MESH,
                    ).start()

                if over or low or twin_core:
                    remote()
                else:
                    here = (x == y) & (n == len(FAR_FIRST) - 1)
                    pl.when(jnp.logical_not(here))(remote)

                    @pl.when(here)
                    def _():
                        pltpu.make_async_copy(tell.at[home], got.at[sender], route_recv.at[0]).start()

        return carry

    lax.fori_loop(0, len(FAR_FIRST), route, 0)

    block = home
    own_ids = members[pl.ds(x, 1), pl.ds(pl.multiple_of(block * MEM, MEM), MEM)]
    shard = own_ids // 2048
    shard_rows = jnp.concatenate([spread(shard[:, :128].astype(F32)), spread(shard[:, 128:].astype(F32))], axis=0)
    shard_rows = jnp.concatenate([shard_rows, shard_rows], axis=1)
    same = (shard_rows == shard.astype(F32)) & (
        lax.broadcasted_iota(jnp.int32, (MEM, MEM), 0) < lax.broadcasted_iota(jnp.int32, (MEM, MEM), 1)
    )
    rank = jnp.sum(jnp.where(same, 1.0, 0.0), axis=0, keepdims=True).astype(jnp.int32)
    from_sender = ((shard // 16) * 8 + shard % 8) * 2 + rank // 2
    from_place = (rank % 2) * 2 + (shard // 8) % 2
    from_which = from_sender * 4 + from_place
    slots = block * MEM + lax.broadcasted_iota(jnp.int32, (1, MEM), 1)
    in_use = slots < sizes[x]
    lane_z = lax.broadcasted_iota(jnp.int32, (4, 128), 1) % 16
    senders = lax.broadcasted_iota(jnp.int32, (64, MEM), 0)

    pltpu.make_async_remote_copy(got, got, route_send.at[0], route_recv.at[0], device_id=at(0, 0, 1), device_id_type=MESH).wait_recv()
    for rr in range(2):
        heard = got[:, rr, :]
        swap[rr] = jnp.transpose(jnp.concatenate([heard, heard], axis=0))
    value = jnp.full((4, 128), -1.0, F32)
    for p in range(len(PARTS)):
        (dx, dz), other = PARTS[p]
        rows = jnp.concatenate([swap[0, 2 * p : 2 * p + 2, :], swap[1, 2 * p : 2 * p + 2, :]], axis=0)
        if dx % 4 or dz % 8:
            turn = 16 * (dx % 4) + 2 * (dz % 8)
            moved = pltpu.roll(rows, turn, 1)
            if dz % 8:
                moved = jnp.where(lane_z >= 2 * (dz % 8), moved, pltpu.roll(rows, (turn - 16) % 128, 1))
            rows = moved
        if other:
            rows = jnp.where(lane_z % 2 == 0, pltpu.roll(rows, 127, 1), pltpu.roll(rows, 1, 1))
        value = jnp.maximum(value, rows)
    final = jnp.zeros((1, MEM), F32)
    for place in range(4):
        column = spread(value[place : place + 1, :])[:64]
        column = jnp.concatenate([column, column], axis=1)
        here = from_which == senders * 4 + place
        final = final + jnp.sum(jnp.where(here, column, 0.0), axis=0, keepdims=True)
    out[...] = jnp.where(in_use, final, 0.0)

    sent = held.at[pl.ds(0, N_SENT)]
    pltpu.make_async_remote_copy(sent, sent, send_sem.at[0], recv_sem.at[0], device_id=at(0, 0, 1), device_id_type=MESH).wait_send()

    @pl.when(x == y)
    def _():
        fewer = got.at[pl.ds(0, 63)]
        pltpu.make_async_remote_copy(fewer, fewer, route_send.at[0], route_recv.at[0], device_id=at(0, 0, 1), device_id_type=MESH).wait_send()

    @pl.when(x != y)
    def _():
        pltpu.make_async_remote_copy(got, got, route_send.at[0], route_recv.at[0], device_id=at(0, 0, 1), device_id_type=MESH).wait_send()


def on_device(embeddings, members, order, sizes):
    vmem = pltpu.VMEM
    dma = pltpu.SemaphoreType.DMA
    best = pl.pallas_call(
        kernel,
        out_shape=jax.ShapeDtypeStruct((1, MEM), F32),
        in_specs=[pl.BlockSpec(memory_space=pltpu.HBM)] * 4,
        out_specs=pl.BlockSpec(memory_space=pltpu.VMEM),
        scratch_shapes=[
            pltpu.SMEM((4,), jnp.int32),
            vmem((2048, D), jnp.bfloat16),
            vmem((4, 16384), jnp.int32),
            vmem((4, 16384), jnp.int32),
            vmem((3, 128, MEM), jnp.int32),
            vmem((max(N_HELD * PIECES, N_SENT), ROWS, D), jnp.bfloat16),
            vmem((HALF, ROWS, D), jnp.bfloat16),
            vmem((128, D), F32),
            vmem((len(RIGHT), 8, 512), F32),
            vmem((len(LEFT), MEM, 128), F32),
            vmem((len(RIGHT) + 1, 8, 512), F32),
            vmem((len(LEFT), MEM, 128), F32),
            vmem((128, 128), F32),
            vmem((64, 2, 128), F32),
            vmem((64, 2, 128), F32),
            vmem((2, 128, 128), F32),
            dma((4,)),
            dma((1,)),
            dma((N_SLOTS * PIECES,)),
            dma((N_SLOTS * 2,)),
            dma((1,)),
            dma((1,)),
            pltpu.SemaphoreType.REGULAR,
        ],
        compiler_params=pltpu.CompilerParams(collective_id=0, has_side_effects=True, vmem_limit_bytes=48 << 20),
        cost_estimate=pl.CostEstimate(flops=8 << 30, bytes_accessed=8 << 20, transcendentals=0),
    )(*[pltpu.with_memory_space_constraint(one, pltpu.HBM) for one in (embeddings, members, order, sizes)])
    return best.reshape(MEM)


def solution(mesh):
    return jax.shard_map(
        on_device,
        mesh=mesh,
        in_specs=(P("store", None), P(), P(), P()),
        out_specs=P(("store", "grid", "row")),
        check_vma=False,
    )
```

```python
import jax
import jax.numpy as jnp
from jax import lax
from jax.experimental import pallas as pl
from jax.experimental.pallas import tpu as pltpu
from jax.sharding import PartitionSpec as P

AT = [(0, 0), (0, -2), (0, -1), (0, 1), (0, 2), (1, 1), (2, 2), (-1, 1), (-1, 2)]
ROUTE = [(2, 2, 2, 2, 2, 2, 2, 2), (0, 0, 0, 0, 0, 0, 0, 0), (0, 0, 0, 0, 0, 0, 0, 0), (8, 8, 8, 8, 8, 8, 3, 8), (3, 3, 3, 3, 3, 3, 3, 3), (8, 8, 8, 8, 8, 8, 8, 8), (3, 3, 3, 3, 3, 3, 3, 3), (7, 7, 7, 7, 7, 7, 7, 7)]
PROGRAM = [
    ("send", 2, 1),
    ("send", 3, 1),
    ("send", 2, 3),
    ("send", 3, 3),
    ("send", 2, 0),
    ("send", 3, 0),
    ("send", 2, 2),
    ("send", 3, 2),
    ("piece", 0, 4),
    ("piece", 2, 1),
    ("piece", 3, 1),
    ("send", 1, 1),
    ("send", 3, 4),
    ("send", 5, 1),
    ("send", 7, 1),
    ("send", 2, 4),
    ("piece", 0, 5),
    ("piece", 2, 3),
    ("piece", 3, 3),
    ("send", 1, 3),
    ("send", 3, 5),
    ("send", 5, 3),
    ("send", 7, 3),
    ("piece", 0, 6),
    ("piece", 2, 0),
    ("piece", 3, 0),
    ("send", 3, 6),
    ("send", 5, 0),
    ("send", 7, 0),
    ("piece", 0, 7),
    ("piece", 2, 2),
    ("piece", 3, 2),
    ("send", 2, 7),
    ("send", 3, 7),
    ("send", 5, 2),
    ("send", 7, 2),
    ("send", 2, 5),
    ("piece", 5, 1),
    ("piece", 7, 1),
    ("send", 8, 1),
    ("piece", 1, 1),
    ("piece", 3, 4),
    ("send", 5, 4),
    ("send", 7, 4),
    ("piece", 5, 3),
    ("piece", 7, 3),
    ("send", 8, 3),
    ("piece", 2, 4),
    ("piece", 3, 5),
    ("send", 1, 4),
    ("send", 5, 5),
    ("send", 7, 5),
    ("send", 1, 0),
    ("piece", 5, 0),
    ("piece", 7, 0),
    ("send", 8, 0),
    ("twin", 0, 0),
    ("twin", 0, 1),
    ("products", ((0, 0, False),)),
    ("piece", 1, 3),
    ("piece", 3, 6),
    ("send", 5, 6),
    ("send", 7, 6),
    ("piece", 5, 2),
    ("piece", 7, 2),
    ("piece", 2, 7),
    ("piece", 3, 7),
    ("send", 1, 7),
    ("send", 5, 7),
    ("send", 7, 7),
    ("send", 2, 6),
    ("piece", 5, 4),
    ("piece", 7, 4),
    ("send", 8, 4),
    ("send", 8, 2),
    ("products", ((3, 0, True),)),
    ("send", 1, 2),
    ("piece", 2, 5),
    ("piece", 8, 1),
    ("send", 4, 1),
    ("send", 6, 1),
    ("piece", 5, 5),
    ("piece", 7, 5),
    ("send", 8, 5),
    ("send", 1, 5),
    ("piece", 1, 4),
    ("piece", 8, 3),
    ("send", 4, 3),
    ("send", 6, 3),
    ("piece", 5, 6),
    ("piece", 7, 6),
    ("piece", 1, 0),
    ("piece", 8, 0),
    ("send", 4, 0),
    ("send", 6, 0),
    ("piece", 5, 7),
    ("piece", 7, 7),
    ("send", 8, 7),
    ("send", 8, 6),
    ("products", ((5, 0, True),)),
    ("send", 4, 6),
    ("piece", 1, 7),
    ("piece", 8, 4),
    ("send", 4, 4),
    ("send", 6, 4),
    ("piece", 4, 1),
    ("piece", 6, 1),
    ("known",),
    ("products", ((7, 0, True),)),
    ("piece", 2, 6),
    ("piece", 8, 2),
    ("send", 1, 6),
    ("send", 4, 2),
    ("send", 6, 2),
    ("piece", 4, 3),
    ("piece", 6, 3),
    ("twin", 5, 0),
    ("twin", 5, 1),
    ("products", ((2, 5, True),)),
    ("piece", 1, 2),
    ("piece", 8, 5),
    ("send", 4, 5),
    ("send", 6, 5),
    ("piece", 4, 0),
    ("piece", 6, 0),
    ("products", ((3, 5, True), (7, 5, False))),
    ("piece", 1, 5),
    ("piece", 8, 7),
    ("send", 4, 7),
    ("send", 6, 7),
    ("piece", 4, 4),
    ("piece", 6, 4),
    ("twin", 2, 0),
    ("twin", 2, 1),
    ("products", ((3, 2, True), (7, 2, True))),
    ("piece", 8, 6),
    ("send", 6, 6),
    ("piece", 1, 6),
    ("piece", 4, 2),
    ("piece", 6, 2),
    ("products", ((8, 2, True), (8, 5, True))),
    ("half", ((6, 0, True), (6, 2, True)), 0),
    ("piece", 4, 6),
    ("piece", 4, 5),
    ("piece", 6, 5),
    ("products", ((1, 5, True),)),
    ("piece", 4, 7),
    ("piece", 6, 7),
    ("products", ((4, 2, True),)),
    ("twin", 1, 0),
    ("twin", 1, 1),
    ("products", ((4, 1, False),)),
    ("piece", 6, 6),
    ("products", ((8, 1, True), (6, 1, False))),
    ("half", ((6, 0, True), (6, 2, True)), 1),
]
D = 768
MEM = 256
BLOCKS = 64
PIECES = len(ROUTE[0])
HALF = PIECES // 2
ROWS = MEM // PIECES
NEVER = float(1 << 20)
MESH = pl.DeviceIdType.MESH
FAR_FIRST = (4, 3, 5, 2, 6, 1, 7, 0)
F32 = jnp.float32
N_SLOTS = len(AT)
PRODUCTS = [one for step in PROGRAM if step[0] == "products" for one in step[1]]
LEFT = sorted({one[0] for one in PRODUCTS})
RIGHT = sorted({one[1] for one in PRODUCTS})
BASE = [s + sum(r < s for r in RIGHT) for s in range(N_SLOTS)]
N_HELD = N_SLOTS + len(RIGHT)
PARTS = [(AT[s], 0) for s in LEFT] + [(AT[s], other) for s in RIGHT for other in (0, 1)]
STEPS = {tuple((a - b) for a, b in zip(AT[s], AT[ROUTE[s - 1][q]])) for s in range(1, N_SLOTS) for q in range(PIECES)}
N_SENT = PIECES * (N_SLOTS - 1) + PIECES * len(RIGHT) + HALF


def coordinates():
    store = lax.axis_index("store")
    return store // 16, (store // 8) % 2, store % 8, lax.axis_index("grid"), lax.axis_index("row")


def device(x, y_hi, z, core, y_lo):
    return (x * 16 + y_hi * 8 + z, core, y_lo)


def spread(row):
    return jnp.transpose(jnp.broadcast_to(row, (128, 128)))


def lookup(n, values):
    if len(set(values)) == 1:
        return values[0]
    found = jnp.int32(values[0])
    for k in range(1, len(values)):
        if values[k] != values[0]:
            found = jnp.where(n == k, jnp.int32(values[k]), found)
    return found


def kernel(emb_hbm, members_hbm, order_hbm, sizes_hbm, out, sizes, emb, members, order, table, held, give, vec, col_ord, row_ord, col_best, row_best, lines, tell, got, swap, load_sem, send_sem, recv_sem, twin_sem, route_send, route_recv, known):
    x, y_hi, z, core, y_lo = coordinates()
    y = y_hi * 2 + y_lo
    store = x * 16 + y_hi * 8 + z

    def at(dx, dz, other=0, across=False):
        side = core if other == 0 else 1 - core
        if across:
            return device((x + dx + 4) % 4, 1 - y_hi, (z + dz + 8) % 8, side, 1 - y_lo)
        return device((x + dx + 4) % 4, y_hi, (z + dz + 8) % 8, side, y_lo)

    near = sorted({((sign * dx) % 4, (sign * dz) % 8) for dx, dz in STEPS for sign in (1, -1)})
    greet = [at(dx, dz) for dx, dz in near] + [at(0, 0, 0, True), at(0, 0, 1)]
    greet += [device(x, y_hi, z, side, 1 - y_lo) for side in (core, 1 - core)]
    greet += [device(x, 1 - y_hi, z, side, y_lo) for side in (core, 1 - core)]
    greet.append(device(x, 1 - y_hi, z, 1 - core, 1 - y_lo))
    barrier = pltpu.get_barrier_semaphore()
    for one in greet:
        pl.semaphore_signal(barrier, inc=1, device_id=one, device_id_type=MESH)

    loads = [
        pltpu.make_async_copy(members_hbm, members, load_sem.at[0]),
        pltpu.make_async_copy(order_hbm, order, load_sem.at[1]),
        pltpu.make_async_copy(emb_hbm, emb, load_sem.at[2]),
        pltpu.make_async_copy(sizes_hbm, sizes, load_sem.at[3]),
    ]
    for one in loads:
        one.start()
    loads[0].wait()

    def lay(ref, cluster, where):
        for b in range(BLOCKS):
            line = ref[pl.ds(cluster, 1), b * MEM : (b + 1) * MEM]
            table[where, b : b + 1, :] = line
            table[where, BLOCKS + b : BLOCKS + b + 1, :] = line

    lay(members, y, 0)
    lay(members, 3 - y, 1)
    ids = jnp.transpose(table[0])
    ids_partner = jnp.transpose(table[1])
    upper = lax.broadcasted_iota(jnp.int32, (1, 128), 1) // BLOCKS
    before = (
        lax.broadcasted_iota(jnp.int32, (MEM, MEM), 1) < lax.broadcasted_iota(jnp.int32, (MEM, MEM), 0)
    ).astype(jnp.bfloat16)

    def ranks(local):
        inside = (local >= 0) & (local < 2048)
        count = jnp.dot(before, jnp.where(inside, 1.0, 0.0).astype(jnp.bfloat16), preferred_element_type=F32)
        return jnp.where(inside, count, -1.0)

    def pick(rank, side, values):
        wanted = (2 * side + upper).astype(F32)
        return jnp.sum(jnp.where(rank == wanted, values, 0.0), axis=0, keepdims=True)

    chosen = []
    for table_ids in (ids_partner, ids):
        local = table_ids - store * 2048
        chosen.append(spread(pick(ranks(local), core, local.astype(F32))).astype(jnp.int32))
    loads[2].wait()
    lane = lax.broadcasted_iota(jnp.int32, (128, 128), 1)
    for half in range(2):
        onehot = jnp.concatenate([jnp.where(chosen[half] == lane + 128 * j, 1.0, 0.0).astype(jnp.bfloat16) for j in range(16)], axis=1)
        for n in range(3):
            vec[:, n * 256 : (n + 1) * 256] = jnp.dot(onehot, emb[:, n * 256 : (n + 1) * 256], preferred_element_type=F32)
        vector = vec[...]
        scale = lax.rsqrt(jnp.sum(vector * vector, axis=1, keepdims=True) + 1e-06)
        unit = (vector * scale).astype(jnp.bfloat16).reshape(HALF, ROWS, D)
        if half == 0:
            give[...] = unit
        else:
            held[pl.ds(y_hi * HALF, HALF)] = unit

    pl.semaphore_wait(barrier, len(greet))

    def side_of(half):
        return y_hi if half == 0 else 1 - y_hi

    def piece(slot, q):
        return BASE[slot] * PIECES + side_of(q // HALF) * HALF + q % HALF

    def push(src, dst, sem, to):
        pltpu.make_async_remote_copy(src, dst, send_sem.at[0], sem, device_id=to, device_id_type=MESH).start()

    def landed(ref, sem):
        pltpu.make_async_remote_copy(ref, ref, send_sem.at[0], sem, device_id=at(0, 0, 1), device_id_type=MESH).wait_recv()

    def send(s, q):
        slot = ROUTE[s - 1][q]
        push(held.at[piece(slot, q)], held.at[piece(s, q)], recv_sem.at[s * PIECES + q], at(AT[slot][0] - AT[s][0], AT[slot][1] - AT[s][1]))

    def twin(slot, half):
        if slot in RIGHT:
            where = BASE[slot] * PIECES + side_of(half) * HALF
            push(held.at[pl.ds(where, HALF)], held.at[pl.ds(where + PIECES, HALF)], twin_sem.at[slot * 2 + half], at(0, 0, 1))

    for q in range(HALF):
        push(give.at[q], held.at[y_hi * HALF + q], recv_sem.at[HALF + q], at(0, 0, 0, True))
    first = [step[0] for step in PROGRAM].index("piece")
    for step in PROGRAM[:first]:
        send(*step[1:])
    twin(0, 0)

    loads[1].wait()
    loads[3].wait()
    lay(order, y, 2)
    slot = lax.broadcasted_iota(jnp.int32, (MEM, 128), 0) + MEM * (lax.broadcasted_iota(jnp.int32, (MEM, 128), 1) % BLOCKS)
    rank_of = jnp.where(slot < sizes[y], jnp.transpose(table[2]).astype(F32), NEVER)
    for s in range(N_SLOTS):
        for hi in range(2):
            shard = ((x + AT[s][0] + 4) % 4) * 16 + hi * 8 + (z + AT[s][1] + 8) % 8
            rank = ranks(ids - shard * 2048)
            line = pick(rank, core, rank_of)
            if s in LEFT:
                row_ord[LEFT.index(s), hi * 128 : (hi + 1) * 128, :] = spread(line)
            if s in RIGHT:
                r = RIGHT.index(s)
                col_ord[r, :, hi * 128 : (hi + 1) * 128] = jnp.broadcast_to(line, (8, 128))
                line = pick(rank, 1 - core, rank_of)
                col_ord[r, :, 256 + hi * 128 : 256 + (hi + 1) * 128] = jnp.broadcast_to(line, (8, 128))
    col_best[...] = jnp.full(col_best.shape, -1.0, F32)
    row_best[...] = jnp.full(row_best.shape, -1.0, F32)

    def half_products(group, half):
        rows = pl.ds(pl.multiple_of(side_of(half) * 128, 128), 128)

        def one(n, carry):
            left = lookup(n, [LEFT.index(a) for a, b, full in group])
            left_at = lookup(n, [BASE[a] * PIECES for a, b, full in group])
            right = lookup(n, [RIGHT.index(b) for a, b, full in group])
            right_at = lookup(n, [BASE[b] * PIECES for a, b, full in group])
            column = lookup(n, [RIGHT.index(b) if full else len(RIGHT) for a, b, full in group])
            a = held[pl.ds(left_at + side_of(half) * HALF, HALF)].reshape(128, D)
            b = held[pl.ds(right_at, 2 * PIECES)].reshape(2 * MEM, D)
            score = lax.dot_general(a, b, (((1,), (1,)), ((), ())), preferred_element_type=F32)
            own = row_ord[left, rows, :]
            best = row_best[left, rows, :]
            for part in range(4):
                lanes = slice(part * 128, (part + 1) * 128)
                mine = score[:, lanes]
                earlier = col_ord[right, 0:1, lanes] < own
                best = jnp.maximum(best, jnp.where(earlier, mine, -1.0))
                later = jnp.max(jnp.where(earlier, -1.0, mine).reshape(16, 8, 128), axis=0)
                col_best[column, :, lanes] = jnp.maximum(col_best[column, :, lanes], later)
            row_best[left, rows, :] = best
            return carry

        lax.fori_loop(0, len(group), one, 0, unroll=True)

    def products(group):
        def one(n, carry):
            left = lookup(n, [LEFT.index(a) for a, b, full in group])
            left_at = lookup(n, [BASE[a] * PIECES for a, b, full in group])
            right = lookup(n, [RIGHT.index(b) for a, b, full in group])
            right_at = lookup(n, [BASE[b] * PIECES for a, b, full in group])
            column = lookup(n, [RIGHT.index(b) if full else len(RIGHT) for a, b, full in group])
            a = held[pl.ds(left_at, PIECES)].reshape(MEM, D)
            b = held[pl.ds(right_at, 2 * PIECES)].reshape(2 * MEM, D)
            score = lax.dot_general(a, b, (((1,), (1,)), ((), ())), preferred_element_type=F32)
            own = row_ord[left]
            best = row_best[left]
            for part in range(4):
                lanes = slice(part * 128, (part + 1) * 128)
                mine = score[:, lanes]
                earlier = col_ord[right, 0:1, lanes] < own
                best = jnp.maximum(best, jnp.where(earlier, mine, -1.0))
                later = jnp.max(jnp.where(earlier, -1.0, mine).reshape(32, 8, 128), axis=0)
                col_best[column, :, lanes] = jnp.maximum(col_best[column, :, lanes], later)
            row_best[left] = best
            return carry

        if len(group) == 1:
            one(0, 0)
        else:
            lax.fori_loop(0, len(group), one, 0, unroll=True)

    for step in PROGRAM[first:]:
        if step[0] == "send":
            send(*step[1:])
        elif step[0] == "piece":
            s, q = step[1:]
            landed(held.at[piece(s, q)], recv_sem.at[s * PIECES + q])
            half = {("piece", s, r) for r in range(PIECES) if r // HALF == q // HALF}
            if half <= set(PROGRAM[: PROGRAM.index(step) + 1]):
                twin(s, q // HALF)
        elif step[0] == "known":
            for s in range(1, N_SLOTS):
                pl.semaphore_signal(known, inc=1, device_id=at(AT[s][0], AT[s][1]), device_id_type=MESH)
        elif step[0] == "twin":
            s, half = step[1:]
            landed(held.at[pl.ds(BASE[s] * PIECES + PIECES + side_of(half) * HALF, HALF)], twin_sem.at[s * 2 + half])
        elif step[0] == "half":
            half_products(*step[1:])
        else:
            products(step[1])

    for p in range(len(PARTS)):
        for hi in range(2):
            if p < len(LEFT):
                line = jnp.max(jnp.transpose(row_best[p, hi * 128 : (hi + 1) * 128, :]), axis=0, keepdims=True)
            else:
                r, other = (p - len(LEFT)) // 2, (p - len(LEFT)) % 2
                line = jnp.max(col_best[r, :, other * 256 + hi * 128 : other * 256 + (hi + 1) * 128], axis=0, keepdims=True)
            lines[p * 2 + hi : p * 2 + hi + 1, :] = line
    turned = jnp.transpose(lines[...])
    tell[:, 0, :] = turned[:BLOCKS]
    tell[:, 1, :] = turned[BLOCKS:]

    pl.semaphore_wait(known, N_SLOTS - 1)

    sender = (x * 8 + z) * 2 + core
    home = (y_hi * 8 + z) * 4 + core * 2 + y_lo

    def route(n, carry):
        to_z = lax.rem(z + lookup(n, FAR_FIRST), 8)
        for over, low in ((1, 0), (1, 1), (0, 1), (0, 0)):
            to_hi = 1 - y_hi if over else y_hi
            to_lo = 1 - y_lo if low else y_lo
            for twin_core in (1, 0):
                to_core = 1 - core if twin_core else core
                store_there = to_hi * 8 + to_z

                def remote():
                    pltpu.make_async_remote_copy(
                        tell.at[store_there * 4 + to_core * 2 + to_lo],
                        got.at[sender],
                        route_send.at[0],
                        route_recv.at[0],
                        device_id=(y * 16 + store_there, to_core, to_lo),
                        device_id_type=MESH,
                    ).start()

                if over or low or twin_core:
                    remote()
                else:
                    here = (x == y) & (n == len(FAR_FIRST) - 1)
                    pl.when(jnp.logical_not(here))(remote)

                    @pl.when(here)
                    def _():
                        pltpu.make_async_copy(tell.at[home], got.at[sender], route_recv.at[0]).start()

        return carry

    lax.fori_loop(0, len(FAR_FIRST), route, 0)

    block = home
    own_ids = members[pl.ds(x, 1), pl.ds(pl.multiple_of(block * MEM, MEM), MEM)]
    shard = own_ids // 2048
    shard_rows = jnp.concatenate([spread(shard[:, :128].astype(F32)), spread(shard[:, 128:].astype(F32))], axis=0)
    shard_rows = jnp.concatenate([shard_rows, shard_rows], axis=1)
    same = (shard_rows == shard.astype(F32)) & (
        lax.broadcasted_iota(jnp.int32, (MEM, MEM), 0) < lax.broadcasted_iota(jnp.int32, (MEM, MEM), 1)
    )
    rank = jnp.sum(jnp.where(same, 1.0, 0.0), axis=0, keepdims=True).astype(jnp.int32)
    from_sender = ((shard // 16) * 8 + shard % 8) * 2 + rank // 2
    from_place = (rank % 2) * 2 + (shard // 8) % 2
    from_which = from_sender * 4 + from_place
    slots = block * MEM + lax.broadcasted_iota(jnp.int32, (1, MEM), 1)
    in_use = slots < sizes[x]
    lane_z = lax.broadcasted_iota(jnp.int32, (4, 128), 1) % 16
    senders = lax.broadcasted_iota(jnp.int32, (64, MEM), 0)

    pltpu.make_async_remote_copy(got, got, route_send.at[0], route_recv.at[0], device_id=at(0, 0, 1), device_id_type=MESH).wait_recv()
    for rr in range(2):
        heard = got[:, rr, :]
        swap[rr] = jnp.transpose(jnp.concatenate([heard, heard], axis=0))
    value = jnp.full((4, 128), -1.0, F32)
    for p in range(len(PARTS)):
        (dx, dz), other = PARTS[p]
        rows = jnp.concatenate([swap[0, 2 * p : 2 * p + 2, :], swap[1, 2 * p : 2 * p + 2, :]], axis=0)
        if dx % 4 or dz % 8:
            turn = 16 * (dx % 4) + 2 * (dz % 8)
            moved = pltpu.roll(rows, turn, 1)
            if dz % 8:
                moved = jnp.where(lane_z >= 2 * (dz % 8), moved, pltpu.roll(rows, (turn - 16) % 128, 1))
            rows = moved
        if other:
            rows = jnp.where(lane_z % 2 == 0, pltpu.roll(rows, 127, 1), pltpu.roll(rows, 1, 1))
        value = jnp.maximum(value, rows)
    final = jnp.zeros((1, MEM), F32)
    for place in range(4):
        column = spread(value[place : place + 1, :])[:64]
        column = jnp.concatenate([column, column], axis=1)
        here = from_which == senders * 4 + place
        final = final + jnp.sum(jnp.where(here, column, 0.0), axis=0, keepdims=True)
    out[...] = jnp.where(in_use, final, 0.0)

    sent = held.at[pl.ds(0, N_SENT)]
    pltpu.make_async_remote_copy(sent, sent, send_sem.at[0], recv_sem.at[0], device_id=at(0, 0, 1), device_id_type=MESH).wait_send()

    @pl.when(x == y)
    def _():
        fewer = got.at[pl.ds(0, 63)]
        pltpu.make_async_remote_copy(fewer, fewer, route_send.at[0], route_recv.at[0], device_id=at(0, 0, 1), device_id_type=MESH).wait_send()

    @pl.when(x != y)
    def _():
        pltpu.make_async_remote_copy(got, got, route_send.at[0], route_recv.at[0], device_id=at(0, 0, 1), device_id_type=MESH).wait_send()


def on_device(embeddings, members, order, sizes):
    vmem = pltpu.VMEM
    dma = pltpu.SemaphoreType.DMA
    best = pl.pallas_call(
        kernel,
        out_shape=jax.ShapeDtypeStruct((1, MEM), F32),
        in_specs=[pl.BlockSpec(memory_space=pltpu.HBM)] * 4,
        out_specs=pl.BlockSpec(memory_space=pltpu.VMEM),
        scratch_shapes=[
            pltpu.SMEM((4,), jnp.int32),
            vmem((2048, D), jnp.bfloat16),
            vmem((4, 16384), jnp.int32),
            vmem((4, 16384), jnp.int32),
            vmem((3, 128, MEM), jnp.int32),
            vmem((max(N_HELD * PIECES, N_SENT), ROWS, D), jnp.bfloat16),
            vmem((HALF, ROWS, D), jnp.bfloat16),
            vmem((128, D), F32),
            vmem((len(RIGHT), 8, 512), F32),
            vmem((len(LEFT), MEM, 128), F32),
            vmem((len(RIGHT) + 1, 8, 512), F32),
            vmem((len(LEFT), MEM, 128), F32),
            vmem((128, 128), F32),
            vmem((64, 2, 128), F32),
            vmem((64, 2, 128), F32),
            vmem((2, 128, 128), F32),
            dma((4,)),
            dma((1,)),
            dma((N_SLOTS * PIECES,)),
            dma((N_SLOTS * 2,)),
            dma((1,)),
            dma((1,)),
            pltpu.SemaphoreType.REGULAR,
        ],
        compiler_params=pltpu.CompilerParams(collective_id=0, has_side_effects=True, vmem_limit_bytes=48 << 20),
        cost_estimate=pl.CostEstimate(flops=8 << 30, bytes_accessed=8 << 20, transcendentals=0),
    )(*[pltpu.with_memory_space_constraint(one, pltpu.HBM) for one in (embeddings, members, order, sizes)])
    return best.reshape(MEM)


def solution(mesh):
    return jax.shard_map(
        on_device,
        mesh=mesh,
        in_specs=(P("store", None), P(), P(), P()),
        out_specs=P(("store", "grid", "row")),
        check_vma=False,
    )
```

```python
import jax
import jax.numpy as jnp
from jax import lax
from jax.experimental import pallas as pl
from jax.experimental.pallas import tpu as pltpu
from jax.sharding import PartitionSpec as P

AT = [(0, 0), (0, -2), (0, -1), (0, 1), (0, 2), (1, 1), (2, 2), (-1, 1), (-1, 2)]
ROUTE = [(2, 2, 2, 2, 2, 2, 2, 2), (0, 0, 0, 0, 0, 0, 0, 0), (0, 0, 0, 0, 0, 0, 0, 0), (8, 8, 8, 8, 8, 8, 3, 8), (3, 3, 3, 3, 3, 3, 3, 3), (8, 8, 8, 8, 8, 8, 8, 8), (3, 3, 3, 3, 3, 3, 3, 3), (7, 7, 7, 7, 7, 7, 7, 7)]
PROGRAM = [
    ("send", 2, 1),
    ("send", 3, 1),
    ("send", 2, 3),
    ("send", 3, 3),
    ("send", 2, 0),
    ("send", 3, 0),
    ("send", 2, 2),
    ("send", 3, 2),
    ("piece", 0, 4),
    ("piece", 2, 1),
    ("piece", 3, 1),
    ("send", 1, 1),
    ("send", 3, 4),
    ("send", 5, 1),
    ("send", 7, 1),
    ("send", 2, 4),
    ("piece", 0, 5),
    ("piece", 2, 3),
    ("piece", 3, 3),
    ("send", 1, 3),
    ("send", 3, 5),
    ("send", 5, 3),
    ("send", 7, 3),
    ("piece", 0, 6),
    ("piece", 2, 0),
    ("piece", 3, 0),
    ("send", 3, 6),
    ("send", 5, 0),
    ("send", 7, 0),
    ("piece", 0, 7),
    ("piece", 2, 2),
    ("piece", 3, 2),
    ("send", 2, 7),
    ("send", 3, 7),
    ("send", 5, 2),
    ("send", 7, 2),
    ("send", 2, 5),
    ("piece", 5, 1),
    ("piece", 7, 1),
    ("send", 8, 1),
    ("piece", 1, 1),
    ("piece", 3, 4),
    ("send", 5, 4),
    ("send", 7, 4),
    ("piece", 5, 3),
    ("piece", 7, 3),
    ("send", 8, 3),
    ("piece", 2, 4),
    ("piece", 3, 5),
    ("send", 1, 4),
    ("send", 5, 5),
    ("send", 7, 5),
    ("send", 1, 0),
    ("piece", 5, 0),
    ("piece", 7, 0),
    ("send", 8, 0),
    ("twin", 0, 0),
    ("twin", 0, 1),
    ("products", ((0, 0, False),)),
    ("piece", 1, 3),
    ("piece", 3, 6),
    ("send", 5, 6),
    ("send", 7, 6),
    ("piece", 5, 2),
    ("piece", 7, 2),
    ("piece", 2, 7),
    ("piece", 3, 7),
    ("send", 1, 7),
    ("send", 5, 7),
    ("send", 7, 7),
    ("send", 2, 6),
    ("piece", 5, 4),
    ("piece", 7, 4),
    ("send", 8, 4),
    ("send", 8, 2),
    ("products", ((3, 0, True),)),
    ("send", 1, 2),
    ("piece", 2, 5),
    ("piece", 8, 1),
    ("send", 4, 1),
    ("send", 6, 1),
    ("piece", 5, 5),
    ("piece", 7, 5),
    ("send", 8, 5),
    ("send", 1, 5),
    ("piece", 1, 4),
    ("piece", 8, 3),
    ("send", 4, 3),
    ("send", 6, 3),
    ("piece", 5, 6),
    ("piece", 7, 6),
    ("piece", 1, 0),
    ("piece", 8, 0),
    ("send", 4, 0),
    ("send", 6, 0),
    ("piece", 5, 7),
    ("piece", 7, 7),
    ("send", 8, 7),
    ("send", 8, 6),
    ("products", ((5, 0, True),)),
    ("send", 4, 6),
    ("piece", 1, 7),
    ("piece", 8, 4),
    ("send", 4, 4),
    ("send", 6, 4),
    ("piece", 4, 1),
    ("piece", 6, 1),
    ("known",),
    ("products", ((7, 0, True),)),
    ("piece", 2, 6),
    ("piece", 8, 2),
    ("send", 1, 6),
    ("send", 4, 2),
    ("send", 6, 2),
    ("piece", 4, 3),
    ("piece", 6, 3),
    ("twin", 5, 0),
    ("twin", 5, 1),
    ("products", ((2, 5, True),)),
    ("piece", 1, 2),
    ("piece", 8, 5),
    ("send", 4, 5),
    ("send", 6, 5),
    ("piece", 4, 0),
    ("piece", 6, 0),
    ("products", ((3, 5, True), (7, 5, False))),
    ("piece", 1, 5),
    ("piece", 8, 7),
    ("send", 4, 7),
    ("send", 6, 7),
    ("piece", 4, 4),
    ("piece", 6, 4),
    ("twin", 2, 0),
    ("twin", 2, 1),
    ("products", ((3, 2, True), (7, 2, True))),
    ("piece", 8, 6),
    ("send", 6, 6),
    ("piece", 1, 6),
    ("piece", 4, 2),
    ("piece", 6, 2),
    ("products", ((8, 2, True), (8, 5, True))),
    ("piece", 4, 6),
    ("piece", 4, 5),
    ("piece", 6, 5),
    ("products", ((1, 5, True),)),
    ("piece", 4, 7),
    ("piece", 6, 7),
    ("products", ((4, 2, True),)),
    ("twin", 1, 0),
    ("twin", 1, 1),
    ("products", ((4, 1, False),)),
    ("piece", 6, 6),
    ("products", ((8, 1, True), (6, 0, True), (6, 1, False), (6, 2, True))),
]
D = 768
MEM = 256
BLOCKS = 64
PIECES = len(ROUTE[0])
HALF = PIECES // 2
ROWS = MEM // PIECES
NEVER = float(1 << 20)
MESH = pl.DeviceIdType.MESH
FAR_FIRST = (4, 3, 5, 2, 6, 1, 7, 0)
F32 = jnp.float32
N_SLOTS = len(AT)
PRODUCTS = [one for step in PROGRAM if step[0] == "products" for one in step[1]]
LEFT = sorted({one[0] for one in PRODUCTS})
RIGHT = sorted({one[1] for one in PRODUCTS})
BASE = [s + sum(r < s for r in RIGHT) for s in range(N_SLOTS)]
N_HELD = N_SLOTS + len(RIGHT)
PARTS = [(AT[s], 0) for s in LEFT] + [(AT[s], other) for s in RIGHT for other in (0, 1)]
STEPS = {tuple((a - b) for a, b in zip(AT[s], AT[ROUTE[s - 1][q]])) for s in range(1, N_SLOTS) for q in range(PIECES)}
N_SENT = PIECES * (N_SLOTS - 1) + PIECES * len(RIGHT) + HALF


def coordinates():
    store = lax.axis_index("store")
    return store // 16, (store // 8) % 2, store % 8, lax.axis_index("grid"), lax.axis_index("row")


def device(x, y_hi, z, core, y_lo):
    return (x * 16 + y_hi * 8 + z, core, y_lo)


def spread(row):
    return jnp.transpose(jnp.broadcast_to(row, (128, 128)))


def lookup(n, values):
    if len(set(values)) == 1:
        return values[0]
    found = jnp.int32(values[0])
    for k in range(1, len(values)):
        if values[k] != values[0]:
            found = jnp.where(n == k, jnp.int32(values[k]), found)
    return found


def kernel(emb_hbm, members_hbm, order_hbm, sizes_hbm, out, sizes, emb, members, order, table, held, give, vec, col_ord, row_ord, col_best, row_best, lines, tell, got, swap, load_sem, send_sem, recv_sem, twin_sem, route_send, route_recv, known):
    x, y_hi, z, core, y_lo = coordinates()
    y = y_hi * 2 + y_lo
    store = x * 16 + y_hi * 8 + z

    def at(dx, dz, other=0, across=False):
        side = core if other == 0 else 1 - core
        if across:
            return device((x + dx + 4) % 4, 1 - y_hi, (z + dz + 8) % 8, side, 1 - y_lo)
        return device((x + dx + 4) % 4, y_hi, (z + dz + 8) % 8, side, y_lo)

    near = sorted({((sign * dx) % 4, (sign * dz) % 8) for dx, dz in STEPS for sign in (1, -1)})
    greet = [at(dx, dz) for dx, dz in near] + [at(0, 0, 0, True), at(0, 0, 1)]
    greet += [device(x, y_hi, z, side, 1 - y_lo) for side in (core, 1 - core)]
    greet += [device(x, 1 - y_hi, z, side, y_lo) for side in (core, 1 - core)]
    greet.append(device(x, 1 - y_hi, z, 1 - core, 1 - y_lo))
    barrier = pltpu.get_barrier_semaphore()
    for one in greet:
        pl.semaphore_signal(barrier, inc=1, device_id=one, device_id_type=MESH)

    loads = [
        pltpu.make_async_copy(members_hbm, members, load_sem.at[0]),
        pltpu.make_async_copy(order_hbm, order, load_sem.at[1]),
        pltpu.make_async_copy(emb_hbm, emb, load_sem.at[2]),
        pltpu.make_async_copy(sizes_hbm, sizes, load_sem.at[3]),
    ]
    for one in loads:
        one.start()
    loads[0].wait()

    def lay(ref, cluster, where):
        for b in range(BLOCKS):
            line = ref[pl.ds(cluster, 1), b * MEM : (b + 1) * MEM]
            table[where, b : b + 1, :] = line
            table[where, BLOCKS + b : BLOCKS + b + 1, :] = line

    lay(members, y, 0)
    lay(members, 3 - y, 1)
    ids = jnp.transpose(table[0])
    ids_partner = jnp.transpose(table[1])
    upper = lax.broadcasted_iota(jnp.int32, (1, 128), 1) // BLOCKS
    before = (
        lax.broadcasted_iota(jnp.int32, (MEM, MEM), 1) < lax.broadcasted_iota(jnp.int32, (MEM, MEM), 0)
    ).astype(jnp.bfloat16)

    def ranks(local):
        inside = (local >= 0) & (local < 2048)
        count = jnp.dot(before, jnp.where(inside, 1.0, 0.0).astype(jnp.bfloat16), preferred_element_type=F32)
        return jnp.where(inside, count, -1.0)

    def pick(rank, side, values):
        wanted = (2 * side + upper).astype(F32)
        return jnp.sum(jnp.where(rank == wanted, values, 0.0), axis=0, keepdims=True)

    chosen = []
    for table_ids in (ids_partner, ids):
        local = table_ids - store * 2048
        chosen.append(spread(pick(ranks(local), core, local.astype(F32))).astype(jnp.int32))
    loads[2].wait()
    lane = lax.broadcasted_iota(jnp.int32, (128, 128), 1)
    for half in range(2):
        onehot = jnp.concatenate([jnp.where(chosen[half] == lane + 128 * j, 1.0, 0.0).astype(jnp.bfloat16) for j in range(16)], axis=1)
        for n in range(3):
            vec[:, n * 256 : (n + 1) * 256] = jnp.dot(onehot, emb[:, n * 256 : (n + 1) * 256], preferred_element_type=F32)
        vector = vec[...]
        scale = lax.rsqrt(jnp.sum(vector * vector, axis=1, keepdims=True) + 1e-06)
        unit = (vector * scale).astype(jnp.bfloat16).reshape(HALF, ROWS, D)
        if half == 0:
            give[...] = unit
        else:
            held[pl.ds(y_hi * HALF, HALF)] = unit

    pl.semaphore_wait(barrier, len(greet))

    def side_of(half):
        return y_hi if half == 0 else 1 - y_hi

    def piece(slot, q):
        return BASE[slot] * PIECES + side_of(q // HALF) * HALF + q % HALF

    def push(src, dst, sem, to):
        pltpu.make_async_remote_copy(src, dst, send_sem.at[0], sem, device_id=to, device_id_type=MESH).start()

    def landed(ref, sem):
        pltpu.make_async_remote_copy(ref, ref, send_sem.at[0], sem, device_id=at(0, 0, 1), device_id_type=MESH).wait_recv()

    def send(s, q):
        slot = ROUTE[s - 1][q]
        push(held.at[piece(slot, q)], held.at[piece(s, q)], recv_sem.at[s * PIECES + q], at(AT[slot][0] - AT[s][0], AT[slot][1] - AT[s][1]))

    def twin(slot, half):
        if slot in RIGHT:
            where = BASE[slot] * PIECES + side_of(half) * HALF
            push(held.at[pl.ds(where, HALF)], held.at[pl.ds(where + PIECES, HALF)], twin_sem.at[slot * 2 + half], at(0, 0, 1))

    for q in range(HALF):
        push(give.at[q], held.at[y_hi * HALF + q], recv_sem.at[HALF + q], at(0, 0, 0, True))
    first = [step[0] for step in PROGRAM].index("piece")
    for step in PROGRAM[:first]:
        send(*step[1:])
    twin(0, 0)

    loads[1].wait()
    loads[3].wait()
    lay(order, y, 2)
    slot = lax.broadcasted_iota(jnp.int32, (MEM, 128), 0) + MEM * (lax.broadcasted_iota(jnp.int32, (MEM, 128), 1) % BLOCKS)
    rank_of = jnp.where(slot < sizes[y], jnp.transpose(table[2]).astype(F32), NEVER)
    for s in range(N_SLOTS):
        for hi in range(2):
            shard = ((x + AT[s][0] + 4) % 4) * 16 + hi * 8 + (z + AT[s][1] + 8) % 8
            rank = ranks(ids - shard * 2048)
            line = pick(rank, core, rank_of)
            if s in LEFT:
                row_ord[LEFT.index(s), hi * 128 : (hi + 1) * 128, :] = spread(line)
            if s in RIGHT:
                r = RIGHT.index(s)
                col_ord[r, :, hi * 128 : (hi + 1) * 128] = jnp.broadcast_to(line, (8, 128))
                line = pick(rank, 1 - core, rank_of)
                col_ord[r, :, 256 + hi * 128 : 256 + (hi + 1) * 128] = jnp.broadcast_to(line, (8, 128))
    col_best[...] = jnp.full(col_best.shape, -1.0, F32)
    row_best[...] = jnp.full(row_best.shape, -1.0, F32)

    def products(group):
        def one(n, carry):
            left = lookup(n, [LEFT.index(a) for a, b, full in group])
            left_at = lookup(n, [BASE[a] * PIECES for a, b, full in group])
            right = lookup(n, [RIGHT.index(b) for a, b, full in group])
            right_at = lookup(n, [BASE[b] * PIECES for a, b, full in group])
            column = lookup(n, [RIGHT.index(b) if full else len(RIGHT) for a, b, full in group])
            a = held[pl.ds(left_at, PIECES)].reshape(MEM, D)
            b = held[pl.ds(right_at, 2 * PIECES)].reshape(2 * MEM, D)
            score = lax.dot_general(a, b, (((1,), (1,)), ((), ())), preferred_element_type=F32)
            own = row_ord[left]
            best = row_best[left]
            for part in range(4):
                lanes = slice(part * 128, (part + 1) * 128)
                mine = score[:, lanes]
                earlier = col_ord[right, 0:1, lanes] < own
                best = jnp.maximum(best, jnp.where(earlier, mine, -1.0))
                later = jnp.max(jnp.where(earlier, -1.0, mine).reshape(32, 8, 128), axis=0)
                col_best[column, :, lanes] = jnp.maximum(col_best[column, :, lanes], later)
            row_best[left] = best
            return carry

        if len(group) == 1:
            one(0, 0)
        else:
            lax.fori_loop(0, len(group), one, 0, unroll=True)

    for step in PROGRAM[first:]:
        if step[0] == "send":
            send(*step[1:])
        elif step[0] == "piece":
            s, q = step[1:]
            landed(held.at[piece(s, q)], recv_sem.at[s * PIECES + q])
            half = {("piece", s, r) for r in range(PIECES) if r // HALF == q // HALF}
            if half <= set(PROGRAM[: PROGRAM.index(step) + 1]):
                twin(s, q // HALF)
        elif step[0] == "known":
            for s in range(1, N_SLOTS):
                pl.semaphore_signal(known, inc=1, device_id=at(AT[s][0], AT[s][1]), device_id_type=MESH)
        elif step[0] == "twin":
            s, half = step[1:]
            landed(held.at[pl.ds(BASE[s] * PIECES + PIECES + side_of(half) * HALF, HALF)], twin_sem.at[s * 2 + half])
        else:
            products(step[1])

    for p in range(len(PARTS)):
        for hi in range(2):
            if p < len(LEFT):
                line = jnp.max(jnp.transpose(row_best[p, hi * 128 : (hi + 1) * 128, :]), axis=0, keepdims=True)
            else:
                r, other = (p - len(LEFT)) // 2, (p - len(LEFT)) % 2
                line = jnp.max(col_best[r, :, other * 256 + hi * 128 : other * 256 + (hi + 1) * 128], axis=0, keepdims=True)
            lines[p * 2 + hi : p * 2 + hi + 1, :] = line
    turned = jnp.transpose(lines[...])
    tell[:, 0, :] = turned[:BLOCKS]
    tell[:, 1, :] = turned[BLOCKS:]

    pl.semaphore_wait(known, N_SLOTS - 1)

    sender = (x * 8 + z) * 2 + core
    home = (y_hi * 8 + z) * 4 + core * 2 + y_lo

    def route(n, carry):
        to_z = lax.rem(z + lookup(n, FAR_FIRST), 8)
        for over, low in ((1, 0), (1, 1), (0, 1), (0, 0)):
            to_hi = 1 - y_hi if over else y_hi
            to_lo = 1 - y_lo if low else y_lo
            for twin_core in (1, 0):
                to_core = 1 - core if twin_core else core
                store_there = to_hi * 8 + to_z

                def remote():
                    pltpu.make_async_remote_copy(
                        tell.at[store_there * 4 + to_core * 2 + to_lo],
                        got.at[sender],
                        route_send.at[0],
                        route_recv.at[0],
                        device_id=(y * 16 + store_there, to_core, to_lo),
                        device_id_type=MESH,
                    ).start()

                if over or low or twin_core:
                    remote()
                else:
                    here = (x == y) & (n == len(FAR_FIRST) - 1)
                    pl.when(jnp.logical_not(here))(remote)

                    @pl.when(here)
                    def _():
                        pltpu.make_async_copy(tell.at[home], got.at[sender], route_recv.at[0]).start()

        return carry

    lax.fori_loop(0, len(FAR_FIRST), route, 0, unroll=True)

    block = home
    own_ids = members[pl.ds(x, 1), pl.ds(pl.multiple_of(block * MEM, MEM), MEM)]
    shard = own_ids // 2048
    shard_rows = jnp.concatenate([spread(shard[:, :128].astype(F32)), spread(shard[:, 128:].astype(F32))], axis=0)
    shard_rows = jnp.concatenate([shard_rows, shard_rows], axis=1)
    same = (shard_rows == shard.astype(F32)) & (
        lax.broadcasted_iota(jnp.int32, (MEM, MEM), 0) < lax.broadcasted_iota(jnp.int32, (MEM, MEM), 1)
    )
    rank = jnp.sum(jnp.where(same, 1.0, 0.0), axis=0, keepdims=True).astype(jnp.int32)
    from_sender = ((shard // 16) * 8 + shard % 8) * 2 + rank // 2
    from_place = (rank % 2) * 2 + (shard // 8) % 2
    from_which = from_sender * 4 + from_place
    slots = block * MEM + lax.broadcasted_iota(jnp.int32, (1, MEM), 1)
    in_use = slots < sizes[x]
    lane_z = lax.broadcasted_iota(jnp.int32, (4, 128), 1) % 16
    senders = lax.broadcasted_iota(jnp.int32, (64, MEM), 0)

    pltpu.make_async_remote_copy(got, got, route_send.at[0], route_recv.at[0], device_id=at(0, 0, 1), device_id_type=MESH).wait_recv()
    for rr in range(2):
        heard = got[:, rr, :]
        swap[rr] = jnp.transpose(jnp.concatenate([heard, heard], axis=0))
    value = jnp.full((4, 128), -1.0, F32)
    for p in range(len(PARTS)):
        (dx, dz), other = PARTS[p]
        rows = jnp.concatenate([swap[0, 2 * p : 2 * p + 2, :], swap[1, 2 * p : 2 * p + 2, :]], axis=0)
        if dx % 4 or dz % 8:
            turn = 16 * (dx % 4) + 2 * (dz % 8)
            moved = pltpu.roll(rows, turn, 1)
            if dz % 8:
                moved = jnp.where(lane_z >= 2 * (dz % 8), moved, pltpu.roll(rows, (turn - 16) % 128, 1))
            rows = moved
        if other:
            rows = jnp.where(lane_z % 2 == 0, pltpu.roll(rows, 127, 1), pltpu.roll(rows, 1, 1))
        value = jnp.maximum(value, rows)
    final = jnp.zeros((1, MEM), F32)
    for place in range(4):
        column = spread(value[place : place + 1, :])[:64]
        column = jnp.concatenate([column, column], axis=1)
        here = from_which == senders * 4 + place
        final = final + jnp.sum(jnp.where(here, column, 0.0), axis=0, keepdims=True)
    out[...] = jnp.where(in_use, final, 0.0)

    sent = held.at[pl.ds(0, N_SENT)]
    pltpu.make_async_remote_copy(sent, sent, send_sem.at[0], recv_sem.at[0], device_id=at(0, 0, 1), device_id_type=MESH).wait_send()

    @pl.when(x == y)
    def _():
        fewer = got.at[pl.ds(0, 63)]
        pltpu.make_async_remote_copy(fewer, fewer, route_send.at[0], route_recv.at[0], device_id=at(0, 0, 1), device_id_type=MESH).wait_send()

    @pl.when(x != y)
    def _():
        pltpu.make_async_remote_copy(got, got, route_send.at[0], route_recv.at[0], device_id=at(0, 0, 1), device_id_type=MESH).wait_send()


def on_device(embeddings, members, order, sizes):
    vmem = pltpu.VMEM
    dma = pltpu.SemaphoreType.DMA
    best = pl.pallas_call(
        kernel,
        out_shape=jax.ShapeDtypeStruct((1, MEM), F32),
        in_specs=[pl.BlockSpec(memory_space=pltpu.HBM)] * 4,
        out_specs=pl.BlockSpec(memory_space=pltpu.VMEM),
        scratch_shapes=[
            pltpu.SMEM((4,), jnp.int32),
            vmem((2048, D), jnp.bfloat16),
            vmem((4, 16384), jnp.int32),
            vmem((4, 16384), jnp.int32),
            vmem((3, 128, MEM), jnp.int32),
            vmem((max(N_HELD * PIECES, N_SENT), ROWS, D), jnp.bfloat16),
            vmem((HALF, ROWS, D), jnp.bfloat16),
            vmem((128, D), F32),
            vmem((len(RIGHT), 8, 512), F32),
            vmem((len(LEFT), MEM, 128), F32),
            vmem((len(RIGHT) + 1, 8, 512), F32),
            vmem((len(LEFT), MEM, 128), F32),
            vmem((128, 128), F32),
            vmem((64, 2, 128), F32),
            vmem((64, 2, 128), F32),
            vmem((2, 128, 128), F32),
            dma((4,)),
            dma((1,)),
            dma((N_SLOTS * PIECES,)),
            dma((N_SLOTS * 2,)),
            dma((1,)),
            dma((1,)),
            pltpu.SemaphoreType.REGULAR,
        ],
        compiler_params=pltpu.CompilerParams(collective_id=0, has_side_effects=True, vmem_limit_bytes=48 << 20),
        cost_estimate=pl.CostEstimate(flops=8 << 30, bytes_accessed=8 << 20, transcendentals=0),
    )(*[pltpu.with_memory_space_constraint(one, pltpu.HBM) for one in (embeddings, members, order, sizes)])
    return best.reshape(MEM)


def solution(mesh):
    return jax.shard_map(
        on_device,
        mesh=mesh,
        in_specs=(P("store", None), P(), P(), P()),
        out_specs=P(("store", "grid", "row")),
        check_vma=False,
    )
```
